768 devices in a mesh: node: 96 (over x, z, y_lo), local: 8 (over y_hi, core).
Axes of the slice: x: 4, y: 8 (y_hi: 4, y_lo: 2; y = y_hi * 2 + y_lo), z: 12, core: 2. Of those that a mesh axis runs over, the one named last changes fastest.
Arguments:
- tokens: bfloat16 [98304, 4096], P(('node', 'local')), may hold values from -6 to 6
- cotangent: bfloat16 [98304, 512], P(('node', 'local')), may hold values from -6 to 6
- codes: bfloat16 [8448, 256], P(('node', 'local')), may hold values from -6 to 6
- scales: bfloat16 [8448], P(('node', 'local')), may hold values from 0.0049743652 to 0.049804688
Outputs:
- keys: bfloat16 [98304, 512], P(('node', 'local'))
- grad_input: bfloat16 [98304, 4096], P(('node', 'local'))
- grad_weight: float32 [8448, 256], P(('node', 'local'))
The draws below stay inside these ranges and needn't reach their ends.
All inputs are finite; a program needn't handle non-finite values.
Results may differ from the reference program's by a relative error of at most 0.015.
Values may be sent and summed in bfloat16 or wider, within the bound.
A program may use at most 64 MiB of HBM per device.

```python
import math
import jax
import jax.numpy as jnp
from jax import lax

D = 4096
KV = 512
TOK_DEV = 128
BLOCK = 256
TOKENS = 98304
BLK_PAD = 8448
N_NODE = 96
N_LOCAL = 8


def block_levels(own_key, shape, split, least, largest):
    level = 1.0
    for dim, shards_of in split:
        draws = jax.random.uniform(jax.random.fold_in(jax.random.fold_in(own_key, 6), dim), (shards_of,), jnp.float32, least / len(split), largest / len(split))
        level = level * jnp.repeat(jnp.exp(draws), shape[dim] // shards_of).reshape((-1,) + (1,) * (len(shape) - 1 - dim))
    return level


def bell_draw(key, dims, width, most, cuts=(), kind=jnp.bfloat16):
    result = width * jax.random.normal(key, dims, jnp.float32)
    if cuts:
        result = result * block_levels(key, dims, cuts, -0.22, 0.18)
    return jnp.clip(result, -most, most).astype(kind)


def setup_inputs(seed: int = 0) -> dict:
    streams_of = jax.random.split(jax.random.key(seed), 5)
    return {
        "tokens": bell_draw(streams_of[0], (TOKENS, D), 1.0, 6.0, ((0, 768),)),
        "cotangent": bell_draw(streams_of[1], (TOKENS, KV), 1.0, 6.0, ((0, 768),)),
        "codes": bell_draw(streams_of[2], (BLK_PAD, BLOCK), 1.0, 6.0, ((0, 768),)),
        "scales": jnp.clip(jnp.exp(math.log(0.049804688) - 2.3038113 * jax.random.uniform(streams_of[3], (BLK_PAD,), jnp.float32) ** block_levels(streams_of[3], (BLK_PAD,), ((0, 768),), -0.2, 0.2)), 0.0049743652, 0.049804688).astype(jnp.bfloat16),
    }


def reference(tokens, cotangent, codes, scales):
    blocks = D * KV // BLOCK
    weight = (codes[:blocks].astype(jnp.float32) * scales[:blocks].astype(jnp.float32)[:, None]).reshape(D, KV).astype(jnp.bfloat16)
    keys = jnp.dot(tokens, weight, preferred_element_type=jnp.float32).astype(jnp.bfloat16)
    grad_input = jnp.dot(cotangent, weight.T, preferred_element_type=jnp.float32).astype(jnp.bfloat16)
    factor = 1.0 / (TOKENS ** 0.5)
    tok_split = tokens.reshape(N_NODE * N_LOCAL, TOK_DEV, D)
    cot_split = cotangent.reshape(N_NODE * N_LOCAL, TOK_DEV, KV)

    def device_step(accum, inner):
        term = jnp.dot(inner[0].T, inner[1], preferred_element_type=jnp.float32) * factor
        term = lax.optimization_barrier(term.astype(jnp.bfloat16)).astype(jnp.float32)
        return accum + term, None

    total, unused = lax.scan(device_step, jnp.zeros((D, KV), jnp.float32), (tok_split, cot_split))
    flat = total.reshape(blocks, BLOCK)
    grad_weight = jnp.concatenate([flat, jnp.zeros((BLK_PAD - blocks, BLOCK), jnp.float32)], axis=0)
    return keys, grad_input, grad_weight
```

```python
import functools

import jax
import jax.numpy as jnp
from jax import lax
from jax.experimental import pallas as pl
from jax.experimental.pallas import tpu as pltpu
from jax.sharding import PartitionSpec as P

NX, NY, NZ = 4, 8, 12
D, KV, T = 4096, 512, 128
HALF = KV // 2
OWN = 11
SLAB = OWN * NY
PLANE = SLAB * NZ
ROWS = PLANE * NX
CH = 512
NCH = D // CH
MESH = pl.DeviceIdType.MESH
F32, BF16 = jnp.float32, jnp.bfloat16


def mod(a, n):
    return lax.rem(a, n)


def kernel(
    factor,
    tok_hbm, cot_hbm, wx, keys, gi, gw,
    tok2, cot2, wpair, stage, ychunk, slab, xslab, zpack, zbuf, w32,
    part, xr, r32, frag, ysend, yrecv, ysum, zsend, zrecv, fin,
    gi32, gsend, grecv, ksend, krecv,
    lsem, sib_s, sib_r, ya_s, ya_r, xa_s, xa_r, za_s, za_r,
    xs_s, xs_r, ys_s, ys_r, zs_s, zs_r,
):
    node = lax.axis_index("node")
    local = lax.axis_index("local")
    x = lax.div(node, NZ * 2)
    z = mod(lax.div(node, 2), NZ)
    k = mod(node, 2) * 4 + lax.div(local, 2)
    c = mod(local, 2)

    def dev(x, z, k, c):
        return ((x * NZ + z) * 2 + lax.div(k, 4), mod(k, 4) * 2 + c)

    sib = dev(x, z, k, 1 - c)
    ydev = [dev(x, z, mod(k + o, NY), c) for o in range(1, NY)]
    xdev = [dev(mod(x + o, NX), z, k, c) for o in range(1, NX)]
    zdev = [dev(x, mod(z + o, NZ), k, c) for o in range(1, NZ)]

    def rc(src, dst, ss, rs, to):
        return pltpu.make_async_remote_copy(
            src_ref=src, dst_ref=dst, send_sem=ss, recv_sem=rs, device_id=to, device_id_type=MESH
        )

    load_tok = pltpu.make_async_copy(tok_hbm, tok2.at[0:T], lsem.at[0])
    load_cot = pltpu.make_async_copy(cot_hbm, cot2.at[0:T], lsem.at[1])
    load_tok.start()
    load_cot.start()

    barrier = pltpu.get_barrier_semaphore()
    partners = [sib] + zdev + ydev + xdev
    for to in partners:
        pl.semaphore_signal(barrier, inc=1, device_id=to, device_id_type=MESH)
    wpair[c] = wx[...]
    frag[...] = jnp.zeros_like(frag)
    ysum[...] = jnp.zeros_like(ysum)
    part[:, D:, :] = jnp.zeros((2, ROWS - D, 128), BF16)
    slab[...] = jnp.zeros_like(slab)
    stage[...] = jnp.zeros_like(stage)
    load_tok.wait()
    load_cot.wait()
    pl.semaphore_wait(barrier, len(partners))

    cw = rc(wpair.at[c], wpair.at[c], sib_s.at[0], sib_r.at[0], sib)
    cw.start()
    cc = rc(cot2.at[0:T], cot2.at[T : 2 * T], sib_s.at[1], sib_r.at[1], sib)
    cc.start()
    ct = rc(tok2.at[0:T], tok2.at[T : 2 * T], sib_s.at[2], sib_r.at[2], sib)
    ct.start()
    cw.wait()
    for r in range(OWN):
        rows = []
        for cc_ in range(2):
            i = 2 * r + cc_
            rows.append(wpair[i // OWN, i % OWN : i % OWN + 1, :])
        stage[r : r + 1, :] = jnp.where(c == 0, rows[0], rows[1])
    ychunk[k] = stage[...].astype(BF16)

    for o in range(1, NY):
        rc(ychunk.at[k], ychunk.at[k], ya_s.at[o - 1], ya_r.at[k], ydev[o - 1]).start()

    cc.wait()
    ct.wait()
    mine = pl.ds(pl.multiple_of(c * HALF, 128), HALF)

    def term_step(j, _):
        at = pl.multiple_of(j * CH, CH)
        a = tok2[:, pl.ds(at, CH)]
        t = lax.dot_general(a, cot2[:, mine], (((0,), (0,)), ((), ())), preferred_element_type=F32)
        t = (t * factor).astype(BF16)
        part[0, pl.ds(at, CH), :] = t[:, :128]
        part[1, pl.ds(at, CH), :] = t[:, 128:]
        return 0

    lax.fori_loop(0, NCH, term_step, 0)

    def plane(x):
        return pl.ds(pl.multiple_of(mod(x, NX) * PLANE, 16), PLANE)

    right, left = xdev[0], xdev[2]
    xsums = [
        rc(part.at[0, plane(x + 2)], xr.at[0], xs_s.at[0], xs_r.at[0], right),
        rc(part.at[1, plane(x + 2)], xr.at[1], xs_s.at[1], xs_r.at[1], left),
        rc(part.at[1, plane(x + 1)], xr.at[2], xs_s.at[2], xs_r.at[2], right),
        rc(part.at[0, plane(x + 3)], xr.at[3], xs_s.at[3], xs_r.at[3], left),
        rc(part.at[0, plane(x + 1)], xr.at[4], xs_s.at[4], xs_r.at[4], right),
        rc(part.at[1, plane(x + 3)], xr.at[5], xs_s.at[5], xs_r.at[5], left),
    ]
    for s in range(4):
        xsums[s].start()

    for o in range(1, NY):
        ks = mod(k + o, NY)
        rc(ychunk.at[ks], ychunk.at[ks], ya_s.at[o - 1], ya_r.at[ks], ydev[o - 1]).wait()
    for j in range(NY):
        slab[OWN * j : OWN * (j + 1), :] = ychunk[j].astype(F32)[:OWN]
    xslab[x] = slab[...].astype(BF16)
    for o in range(1, NX):
        rc(xslab.at[x], xslab.at[x], xa_s.at[o - 1], xa_r.at[x], xdev[o - 1]).start()
    for o in range(1, NX):
        xs = mod(x + o, NX)
        rc(xslab.at[xs], xslab.at[xs], xa_s.at[o - 1], xa_r.at[xs], xdev[o - 1]).wait()
    for q in range(2):
        zpack[0:SLAB, :] = xslab[2 * q].astype(F32)[:SLAB]
        zpack[SLAB : 2 * SLAB, :] = xslab[2 * q + 1].astype(F32)[:SLAB]
        zbuf[z, q] = zpack[...].astype(BF16)

    zright, zleft = zdev[0], zdev[NZ - 2]

    def zcopy(way, t, q):
        at = mod(z + (NZ - (t - 1) if way == 0 else t - 1), NZ)
        return rc(
            zbuf.at[at, q], zbuf.at[at, q], za_s.at[way, t - 1, q], za_r.at[at, q],
            zright if way == 0 else zleft,
        )

    def zarrived(way, t, q):
        at = mod(z + (NZ - t if way == 0 else t), NZ)
        rc(
            zbuf.at[at, q], zbuf.at[at, q], za_s.at[way, t - 1, q], za_r.at[at, q],
            zright if way == 0 else zleft,
        ).wait_recv()

    def zmoves(t):
        if t < 6:
            return [(0, 0), (1, 0), (0, 1), (1, 1)]
        return [(0, 0), (1, 1)]

    def place(at, q):
        v = zbuf[at, q].astype(F32)
        for e in range(2):
            to = pl.multiple_of((2 * q + e) * PLANE + at * SLAB, 8)
            w32[pl.ds(to, SLAB), :] = v[e * SLAB : (e + 1) * SLAB]

    def zstep(t):
        for way, q in zmoves(t):
            zarrived(way, t, q)
            if t < 6 and (way, q) in zmoves(t + 1):
                zcopy(way, t + 1, q).start()
        for way, q in zmoves(t):
            place(mod(z + (NZ - t if way == 0 else t), NZ), q)

    for way, q in zmoves(1):
        zcopy(way, 1, q).start()
    for q in range(2):
        place(z, q)
    zstep(1)

    def hand_on(s, h, p):
        xsums[s].wait_recv()
        start = mod(x + p, NX) * PLANE

        def add(j, _):
            rows = pl.ds(pl.multiple_of(start + j * 96, 16), 96)
            got = xr[s, pl.ds(pl.multiple_of(j * 96, 16), 96), :].astype(F32)
            part[h, rows, :] = (part[h, rows, :].astype(F32) + got).astype(BF16)
            return 0

        lax.fori_loop(0, PLANE // 96, add, 0)
        xsums[s + 4].start()

    hand_on(0, 0, 1)
    hand_on(1, 1, 3)
    zstep(2)
    zstep(3)
    for s in (2, 3, 4, 5):
        xsums[s].wait_recv()

    def root(j, _):
        at = pl.multiple_of(j * 96, 16)
        rows = pl.ds(at, 96)
        own = pl.ds(pl.multiple_of(x * PLANE + at, 16), 96)
        a = part[0, own, :].astype(F32) + xr[3, rows, :].astype(F32) + xr[4, rows, :].astype(F32)
        b = part[1, own, :].astype(F32) + xr[2, rows, :].astype(F32) + xr[5, rows, :].astype(F32)
        r32[rows, 0:128] = a
        r32[rows, 128:256] = b
        return 0

    lax.fori_loop(0, PLANE // 96, root, 0)

    def cut(zz, _):
        view = r32.at[pl.ds(pl.multiple_of(zz * 4 * SLAB, 8), 4 * SLAB)]
        for kk in range(NY):
            for i in range(4):
                at = SLAB * i + OWN * kk
                frag[kk, OWN * i : OWN * (i + 1), :] = view[at : at + OWN, :]
        for kk in range(NY):
            ysend[kk, zz] = frag[kk].astype(BF16)
        return 0

    lax.fori_loop(0, 3, cut, 0)
    for o in range(1, NY):
        kt = mod(k + o, NY)
        rc(ysend.at[kt], yrecv.at[k], ys_s.at[o - 1], ys_r.at[k], ydev[o - 1]).start()
    yrecv[k] = ysend[k]

    zstep(4)
    zstep(5)
    zstep(6)

    for o in range(1, NY):
        ks = mod(k + o, NY)
        rc(ysend.at[ks], yrecv.at[ks], ys_s.at[o - 1], ys_r.at[ks], ydev[o - 1]).wait()
    for zz in range(3):
        s = yrecv[0, zz].astype(F32)
        for kk in range(1, NY):
            s = s + yrecv[kk, zz].astype(F32)
        ysum[0:48, :] = s
        for i in range(4):
            zsend[4 * zz + i] = ysum[OWN * i : OWN * i + 16, :].astype(BF16)
    for o in range(1, NZ):
        zt = mod(z + o, NZ)
        rc(zsend.at[zt], zrecv.at[z], zs_s.at[o - 1], zs_r.at[z], zdev[o - 1]).start()
    zrecv[z] = zsend[z]

    def out_step(j, acc):
        at = pl.multiple_of(j * CH, CH)
        w = w32[pl.ds(at, CH), :].astype(BF16)
        acc = acc + jnp.dot(tok2[:, pl.ds(at, CH)], w, preferred_element_type=F32)
        g = lax.dot_general(cot2[:, mine], w, (((1,), (1,)), ((), ())), preferred_element_type=F32)
        gi32[j] = g[:T]
        gsend[j] = g[T:].astype(BF16)
        rc(gsend.at[j], grecv.at[j], sib_s.at[5 + j], sib_r.at[5 + j], sib).start()
        return acc

    acc = lax.fori_loop(0, NCH, out_step, jnp.zeros((2 * T, HALF), F32))
    other = pl.ds(pl.multiple_of((1 - c) * HALF, 128), HALF)
    keys[:, mine] = acc[:T].astype(BF16)
    ksend[...] = acc[T:].astype(BF16)
    ck = rc(ksend, krecv, sib_s.at[3], sib_r.at[3], sib)
    ck.start()

    def join(j, _):
        rc(gsend.at[j], grecv.at[j], sib_s.at[5 + j], sib_r.at[5 + j], sib).wait()
        at = pl.multiple_of(j * CH, CH)
        gi[:, pl.ds(at, CH)] = (gi32[j] + grecv[j].astype(F32)).astype(BF16)
        return 0

    lax.fori_loop(0, NCH, join, 0)
    ck.wait()
    keys[:, other] = krecv[...]

    for o in range(1, NZ):
        zs = mod(z + o, NZ)
        rc(zsend.at[zs], zrecv.at[zs], zs_s.at[o - 1], zs_r.at[zs], zdev[o - 1]).wait()
    s = zrecv[0].astype(F32)
    for j in range(1, NZ):
        s = s + zrecv[j].astype(F32)
    fin[c] = s
    cf = rc(fin.at[c], fin.at[c], sib_s.at[4], sib_r.at[4], sib)
    cf.start()

    for t in range(1, 7):
        for way, q in zmoves(t):
            zcopy(way, t, q).wait_send()
    for s in range(6):
        xsums[s].wait_send()
    cf.wait()
    for r in range(OWN):
        rows = []
        for cc_ in range(2):
            i = OWN * cc_ + r
            rows.append(fin[i % 2, i // 2 : i // 2 + 1, :])
        gw[r : r + 1, :] = jnp.where(c == 0, rows[0], rows[1])


def per_device(tokens, cotangent, codes, scales):
    total = tokens.shape[0] * lax.axis_size("node") * lax.axis_size("local")
    wx = codes.astype(F32) * scales.astype(F32)[:, None]
    wx = jnp.pad(wx, ((0, 16 - OWN), (0, 0)))
    dma = pltpu.SemaphoreType.DMA
    scratch = [
        pltpu.VMEM((2 * T, D), BF16),
        pltpu.VMEM((2 * T, KV), BF16),
        pltpu.VMEM((2, 16, HALF), F32),
        pltpu.VMEM((16, HALF), F32),
        pltpu.VMEM((NY, 16, HALF), BF16),
        pltpu.VMEM((96, HALF), F32),
        pltpu.VMEM((NX, 96, HALF), BF16),
        pltpu.VMEM((2 * SLAB, HALF), F32),
        pltpu.VMEM((NZ, 2, 2 * SLAB, HALF), BF16),
        pltpu.VMEM((ROWS, HALF), F32),
        pltpu.VMEM((2, ROWS, 128), BF16),
        pltpu.VMEM((6, PLANE, 128), BF16),
        pltpu.VMEM((PLANE, HALF), F32),
        pltpu.VMEM((NY, 48, HALF), F32),
        pltpu.VMEM((NY, 3, 48, HALF), BF16),
        pltpu.VMEM((NY, 3, 48, HALF), BF16),
        pltpu.VMEM((56, HALF), F32),
        pltpu.VMEM((NZ, 16, HALF), BF16),
        pltpu.VMEM((NZ, 16, HALF), BF16),
        pltpu.VMEM((2, 16, HALF), F32),
        pltpu.VMEM((NCH, T, CH), F32),
        pltpu.VMEM((NCH, T, CH), BF16),
        pltpu.VMEM((NCH, T, CH), BF16),
        pltpu.VMEM((T, HALF), BF16),
        pltpu.VMEM((T, HALF), BF16),
        dma((2,)),
        dma((5 + NCH,)), dma((5 + NCH,)),
        dma((NY - 1,)), dma((NY,)),
        dma((NX - 1,)), dma((NX,)),
        dma((2, 6, 2)), dma((NZ, 2)),
        dma((6,)), dma((6,)),
        dma((NY - 1,)), dma((NY,)),
        dma((NZ - 1,)), dma((NZ,)),
    ]
    vmem = pl.BlockSpec(memory_space=pltpu.VMEM)
    hbm = pl.BlockSpec(memory_space=pl.ANY)
    return pl.pallas_call(
        functools.partial(kernel, 1.0 / total**0.5),
        out_shape=(
            jax.ShapeDtypeStruct((T, KV), BF16),
            jax.ShapeDtypeStruct((T, D), BF16),
            jax.ShapeDtypeStruct((OWN, HALF), F32),
        ),
        in_specs=[hbm, hbm, vmem],
        out_specs=(vmem, vmem, vmem),
        scratch_shapes=scratch,
        compiler_params=pltpu.CompilerParams(
            collective_id=0, has_side_effects=True, vmem_limit_bytes=44 << 20
        ),
        name="fused",
    )(tokens, cotangent, wx)


def solution(mesh):
    in_specs = (
        P(("node", "local"), None),
        P(("node", "local"), None),
        P(("node", "local"), None),
        P(("node", "local")),
    )
    out_specs = (P(("node", "local"), None), P(("node", "local"), None), P(("node", "local"), None))
    return jax.shard_map(
        per_device, mesh=mesh, in_specs=in_specs, out_specs=out_specs, check_vma=False
    )
```

```python
import functools

import jax
import jax.numpy as jnp
from jax import lax
from jax.experimental import pallas as pl
from jax.experimental.pallas import tpu as pltpu
from jax.sharding import PartitionSpec as P

NX, NY, NZ = 4, 8, 12
D, KV, T = 4096, 512, 128
HALF = KV // 2
OWN = 11
SLAB = OWN * NY
PLANE = SLAB * NZ
ROWS = PLANE * NX
PAD = ROWS - D
PIECE = 4 * SLAB
CH = 512
NCH = D // CH
MESH = pl.DeviceIdType.MESH
F32, BF16 = jnp.float32, jnp.bfloat16


def mod(a, n):
    return lax.rem(a, n)


def kernel(
    factor,
    tok_hbm, cot_hbm, codes_hbm, scales_hbm, keys, gi, gw,
    tok2, cot2, wpair, stage, ychunk, slab, xslab, zpack, zbuf, w32,
    part, xr, r32, frag, ysend, yrecv, ysum, zsend, zrecv, fin,
    gi32, gsend, grecv, ksend, krecv, codes, scales,
    lsem, sib_s, sib_r, ya_s, ya_r, xa_s, xa_r, za_s, za_r, zy_s, zy_r,
    xs_s, xs_r, ys_s, ys_r, zs_s, zs_r,
):
    node = lax.axis_index("node")
    local = lax.axis_index("local")
    x = lax.div(node, NZ * 2)
    z = mod(lax.div(node, 2), NZ)
    k = mod(node, 2) * 4 + lax.div(local, 2)
    y = lax.div(local, 2) * 2 + mod(node, 2)
    c = mod(local, 2)
    odd = mod(node, 2)

    def dev(x, z, k, c):
        return ((x * NZ + z) * 2 + lax.div(k, 4), mod(k, 4) * 2 + c)

    def at_y(y):
        y = mod(y, NY)
        return dev(x, z, mod(y, 2) * 4 + lax.div(y, 2), c)

    sib = dev(x, z, k, 1 - c)
    ydev = [dev(x, z, mod(k + o, NY), c) for o in range(1, NY)]
    xdev = [dev(mod(x + o, NX), z, k, c) for o in range(1, NX)]
    zdev = [dev(x, mod(z + o, NZ), k, c) for o in range(1, NZ)]
    right, left = xdev[0], xdev[2]
    zright, zleft = zdev[0], zdev[NZ - 2]
    up, down = at_y(y + 1), at_y(y + NY - 1)

    def rc(src, dst, ss, rs, to):
        return pltpu.make_async_remote_copy(
            src_ref=src, dst_ref=dst, send_sem=ss, recv_sem=rs, device_id=to, device_id_type=MESH
        )

    barrier = pltpu.get_barrier_semaphore()
    partners = [sib] + zdev + ydev + xdev
    for to in partners:
        pl.semaphore_signal(barrier, inc=1, device_id=to, device_id_type=MESH)
    load_cot = pltpu.make_async_copy(cot_hbm, cot2.at[0:T], lsem.at[1])
    load_tok = pltpu.make_async_copy(tok_hbm, tok2.at[0:T, 0:D], lsem.at[0])
    load_codes = pltpu.make_async_copy(codes_hbm, codes, lsem.at[2])
    load_scales = pltpu.make_async_copy(scales_hbm, scales, lsem.at[3])
    for load in (load_scales, load_codes, load_cot, load_tok):
        load.start()
    frag[...] = jnp.zeros_like(frag)
    ysum[...] = jnp.zeros_like(ysum)
    tok2[:, D:] = jnp.zeros((2 * T, PAD), BF16)
    slab[...] = jnp.zeros_like(slab)
    stage[...] = jnp.zeros_like(stage)
    load_scales.wait()
    load_codes.wait()
    eye = lax.broadcasted_iota(jnp.int32, (OWN, OWN), 0) == lax.broadcasted_iota(
        jnp.int32, (OWN, OWN), 1
    )
    row = jnp.broadcast_to(scales[...].astype(F32), (OWN, OWN))
    column = jnp.sum(jnp.where(eye, row, 0.0), axis=1, keepdims=True)
    wpair[c, 0:OWN, :] = codes[...].astype(F32) * column
    load_cot.wait()
    load_tok.wait()
    pl.semaphore_wait(barrier, len(partners))

    cw = rc(wpair.at[c], wpair.at[c], sib_s.at[0], sib_r.at[0], sib)
    cw.start()
    cc = rc(cot2.at[0:T], cot2.at[T : 2 * T], sib_s.at[1], sib_r.at[1], sib)
    cc.start()
    ct = rc(tok2.at[0:T, 0:D], tok2.at[T : 2 * T, 0:D], sib_s.at[2], sib_r.at[2], sib)
    ct.start()
    cw.wait()
    for r in range(OWN):
        rows = []
        for e in range(2):
            i = 2 * r + e
            rows.append(wpair[i // OWN, i % OWN : i % OWN + 1, :])
        stage[r : r + 1, :] = jnp.where(c == 0, rows[0], rows[1])
    ychunk[k] = stage[...].astype(BF16)

    for o in range(1, NY):
        rc(ychunk.at[k], ychunk.at[k], ya_s.at[o - 1], ya_r.at[k], ydev[o - 1]).start()

    cc.wait()
    ct.wait()
    mine = pl.ds(pl.multiple_of(c * HALF, 128), HALF)

    def term(p):
        def step(j, _):
            at = pl.multiple_of(p * 1024 + j * 384, 128)
            t = lax.dot_general(
                tok2[:, pl.ds(at, 384)], cot2[:, mine], (((0,), (0,)), ((), ())),
                preferred_element_type=F32,
            )
            t = (t * factor).astype(BF16)
            to = pl.ds(pl.multiple_of(j * 384, 16), 384)
            part[p, 0, to, :] = t[:, :128]
            part[p, 1, to, :] = t[:, 128:]
            return 0

        lax.fori_loop(0, 3, step, 0)

    def piece(p, zz):
        return pl.ds(pl.multiple_of(p * 32 + zz * PIECE, 16), PIECE)

    pr, pf, pl_ = mod(x + 1, NX), mod(x + 2, NX), mod(x + 3, NX)

    def xsum(s, zz):
        p, h, to = [
            (pf, 0, right), (pf, 1, left), (pr, 1, right), (pl_, 0, left), (pr, 0, right), (pl_, 1, left),
        ][s]
        return rc(
            part.at[p, h, piece(p, zz)], xr.at[s, zz], xs_s.at[s, zz], xs_r.at[s, zz], to
        )

    def far(zz):
        xsum(0, zz).start()
        xsum(1, zz).start()

    def near(zz):
        xsum(2, zz).start()
        xsum(3, zz).start()

    def hand_on(zz):
        for s, h, p in ((0, 0, pr), (1, 1, pl_)):
            xsum(s, zz).wait_recv()
            rows = piece(p, zz)
            part[p, h, rows, :] = (
                part[p, h, rows, :].astype(F32) + xr[s, zz].astype(F32)
            ).astype(BF16)
            xsum(s + 4, zz).start()

    def root(zz):
        for s in (2, 3, 4, 5):
            xsum(s, zz).wait_recv()
        own = piece(x, zz)
        r32[:, 0:128] = part[x, 0, own, :].astype(F32) + (
            xr[3, zz].astype(F32) + xr[4, zz].astype(F32)
        )
        r32[:, 128:256] = part[x, 1, own, :].astype(F32) + (
            xr[2, zz].astype(F32) + xr[5, zz].astype(F32)
        )
        for kk in range(NY):
            for i in range(4):
                at = SLAB * i + OWN * kk
                frag[kk, OWN * i : OWN * (i + 1), :] = r32[at : at + OWN, :]
        for kk in range(NY):
            ysend[zz, kk] = frag[kk].astype(BF16)
        for o in range(1, NY):
            kt = mod(k + o, NY)
            rc(
                ysend.at[zz, kt], yrecv.at[zz, k], ys_s.at[zz, o - 1], ys_r.at[zz, k], ydev[o - 1]
            ).start()
        yrecv[zz, k] = ysend[zz, k]

    def zsum(zz):
        for o in range(1, NY):
            ks = mod(k + o, NY)
            rc(
                ysend.at[zz, ks], yrecv.at[zz, ks], ys_s.at[zz, o - 1], ys_r.at[zz, ks], ydev[o - 1]
            ).wait()
        s = yrecv[zz, 0].astype(F32)
        for kk in range(1, NY):
            s = s + yrecv[zz, kk].astype(F32)
        ysum[0:48, :] = s
        for i in range(4):
            zt = 4 * zz + i
            zsend[zt] = ysum[OWN * i : OWN * i + 16, :].astype(BF16)

            @pl.when(zt != z)
            def _():
                rc(zsend.at[zt], zrecv.at[z], zs_s.at[zt], zs_r.at[z], dev(x, zt, k, c)).start()

            @pl.when(zt == z)
            def _():
                zrecv[zt] = zsend[zt]

    term(pf)
    far(0)
    term(pr)
    term(pl_)
    near(0)
    term(x)

    for o in range(1, NY):
        ks = mod(k + o, NY)
        rc(ychunk.at[ks], ychunk.at[ks], ya_s.at[o - 1], ya_r.at[ks], ydev[o - 1]).wait()
    for j in range(NY):
        slab[OWN * j : OWN * (j + 1), :] = ychunk[j].astype(F32)[:OWN]
    xslab[x] = slab[...].astype(BF16)
    for o in range(1, NX):
        rc(xslab.at[x], xslab.at[x], xa_s.at[o - 1], xa_r.at[x], xdev[o - 1]).start()
    far(1)
    hand_on(0)
    near(1)
    far(2)
    for o in range(1, NX):
        xs = mod(x + o, NX)
        rc(xslab.at[xs], xslab.at[xs], xa_s.at[o - 1], xa_r.at[xs], xdev[o - 1]).wait()
    for q in range(2):
        zpack[0:SLAB, :] = xslab[2 * q].astype(F32)[:SLAB]
        zpack[SLAB : 2 * SLAB, :] = xslab[2 * q + 1].astype(F32)[:SLAB]
        for h in range(2):
            zbuf[z, q, h] = zpack[:, 128 * h : 128 * h + 128].astype(BF16)

    def zslot(way, t):
        return mod(z + (NZ - t if way == 0 else t), NZ)

    def zhalves(way, t):
        return (0, 1) if t < 6 else (way,)

    def zcopy(way, t, h):
        at = zslot(way, t - 1)
        return rc(
            zbuf.at[at, odd, h], zbuf.at[at, odd, h], za_s.at[way, t - 1, h], za_r.at[at, h],
            zright if way == 0 else zleft,
        )

    def zarrived(way, t, h):
        at = zslot(way, t)
        rc(
            zbuf.at[at, odd, h], zbuf.at[at, odd, h], za_s.at[way, t - 1, h], za_r.at[at, h],
            zright if way == 0 else zleft,
        ).wait_recv()

    def across(way, t, h, q):
        at = zslot(way, t)
        return rc(
            zbuf.at[at, q, h], zbuf.at[at, q, h], zy_s.at[at, h], zy_r.at[at, h],
            up if h == 0 else down,
        )

    def place(at, q, h):
        v = zbuf[at, q, h].astype(F32)
        for e in range(2):
            to = pl.multiple_of((2 * q + e) * PLANE + at * SLAB, 8)
            w32[pl.ds(to, SLAB), 128 * h : 128 * h + 128] = v[e * SLAB : (e + 1) * SLAB]

    def zstep(t):
        for h in range(2):
            for way in range(2):
                if h not in zhalves(way, t):
                    continue
                zarrived(way, t, h)
                if t < 6 and h in zhalves(way, t + 1):
                    zcopy(way, t + 1, h).start()
                across(way, t, h, odd).start()
        for h in range(2):
            for way in range(2):
                if h in zhalves(way, t):
                    place(zslot(way, t), odd, h)

    def from_y(t):
        for h in range(2):
            for way in range(2):
                if h in zhalves(way, t):
                    across(way, t, h, 1 - odd).wait_recv()
                    place(zslot(way, t), 1 - odd, h)

    for h in range(2):
        for way in range(2):
            zcopy(way, 1, h).start()
    for q in range(2):
        for h in range(2):
            place(z, q, h)
    hand_on(1)
    near(2)
    zstep(1)
    root(0)
    zstep(2)
    hand_on(2)
    zstep(3)
    from_y(1)
    root(1)
    zstep(4)
    from_y(2)
    zsum(0)
    zstep(5)
    from_y(3)
    root(2)
    zstep(6)
    from_y(4)
    zsum(1)
    from_y(5)
    from_y(6)
    zsum(2)

    def out_step(j, acc):
        at = pl.multiple_of(j * CH, CH)
        w = w32[pl.ds(at, CH), :].astype(BF16)
        acc = acc + jnp.dot(tok2[:, pl.ds(at, CH)], w, preferred_element_type=F32)
        g = lax.dot_general(cot2[:, mine], w, (((1,), (1,)), ((), ())), preferred_element_type=F32)
        gi32[j] = g[:T]
        gsend[j] = g[T:].astype(BF16)
        rc(gsend.at[j], grecv.at[j], sib_s.at[5 + j], sib_r.at[5 + j], sib).start()
        return acc

    acc = lax.fori_loop(0, NCH, out_step, jnp.zeros((2 * T, HALF), F32))
    other = pl.ds(pl.multiple_of((1 - c) * HALF, 128), HALF)
    keys[:, mine] = acc[:T].astype(BF16)
    ksend[...] = acc[T:].astype(BF16)
    ck = rc(ksend, krecv, sib_s.at[3], sib_r.at[3], sib)
    ck.start()

    def join(j, _):
        rc(gsend.at[j], grecv.at[j], sib_s.at[5 + j], sib_r.at[5 + j], sib).wait()
        at = pl.multiple_of(j * CH, CH)
        gi[:, pl.ds(at, CH)] = (gi32[j] + grecv[j].astype(F32)).astype(BF16)
        return 0

    lax.fori_loop(0, NCH, join, 0)
    ck.wait()
    keys[:, other] = krecv[...]

    for o in range(1, NZ):
        zs = mod(z + o, NZ)
        rc(zsend.at[zs], zrecv.at[zs], zs_s.at[zs], zs_r.at[zs], zdev[o - 1]).wait()
    s = zrecv[0].astype(F32)
    for j in range(1, NZ):
        s = s + zrecv[j].astype(F32)
    fin[c] = s
    cf = rc(fin.at[c], fin.at[c], sib_s.at[4], sib_r.at[4], sib)
    cf.start()

    for t in range(1, 7):
        for way in range(2):
            for h in zhalves(way, t):
                zcopy(way, t, h).wait_send()
                across(way, t, h, odd).wait_send()
    for s in range(6):
        for zz in range(3):
            xsum(s, zz).wait_send()
    cf.wait()
    for r in range(OWN):
        rows = []
        for e in range(2):
            i = OWN * e + r
            rows.append(fin[i % 2, i // 2 : i // 2 + 1, :])
        gw[r : r + 1, :] = jnp.where(c == 0, rows[0], rows[1])


def store(keys, gi, gw, keys_out, gi_out, gw_out, sem):
    copies = [
        pltpu.make_async_copy(gi, gi_out, sem.at[0]),
        pltpu.make_async_copy(keys, keys_out, sem.at[1]),
        pltpu.make_async_copy(gw, gw_out, sem.at[2]),
    ]
    for copy in copies:
        copy.start()
    for copy in copies:
        copy.wait()


def per_device(tokens, cotangent, codes, scales):
    total = tokens.shape[0] * lax.axis_size("node") * lax.axis_size("local")
    dma = pltpu.SemaphoreType.DMA
    scratch = [
        pltpu.VMEM((2 * T, ROWS), BF16),
        pltpu.VMEM((2 * T, KV), BF16),
        pltpu.VMEM((2, 16, HALF), F32),
        pltpu.VMEM((16, HALF), F32),
        pltpu.VMEM((NY, 16, HALF), BF16),
        pltpu.VMEM((96, HALF), F32),
        pltpu.VMEM((NX, 96, HALF), BF16),
        pltpu.VMEM((2 * SLAB, HALF), F32),
        pltpu.VMEM((NZ, 2, 2, 2 * SLAB, 128), BF16),
        pltpu.VMEM((ROWS, HALF), F32),
        pltpu.VMEM((NX, 2, 1152, 128), BF16),
        pltpu.VMEM((6, 3, PIECE, 128), BF16),
        pltpu.VMEM((PIECE, HALF), F32),
        pltpu.VMEM((NY, 48, HALF), F32),
        pltpu.VMEM((3, NY, 48, HALF), BF16),
        pltpu.VMEM((3, NY, 48, HALF), BF16),
        pltpu.VMEM((56, HALF), F32),
        pltpu.VMEM((NZ, 16, HALF), BF16),
        pltpu.VMEM((NZ, 16, HALF), BF16),
        pltpu.VMEM((2, 16, HALF), F32),
        pltpu.VMEM((NCH, T, CH), F32),
        pltpu.VMEM((NCH, T, CH), BF16),
        pltpu.VMEM((NCH, T, CH), BF16),
        pltpu.VMEM((T, HALF), BF16),
        pltpu.VMEM((T, HALF), BF16),
        pltpu.VMEM((OWN, HALF), BF16),
        pltpu.VMEM((1, OWN), BF16),
        dma((4,)),
        dma((5 + NCH,)), dma((5 + NCH,)),
        dma((NY - 1,)), dma((NY,)),
        dma((NX - 1,)), dma((NX,)),
        dma((2, 6, 2)), dma((NZ, 2)), dma((NZ, 2)), dma((NZ, 2)),
        dma((6, 3)), dma((6, 3)),
        dma((3, NY - 1)), dma((3, NY)),
        dma((NZ,)), dma((NZ,)),
    ]
    vmem = pl.BlockSpec(memory_space=pltpu.VMEM)
    hbm = pl.BlockSpec(memory_space=pl.ANY)
    arrays = (tokens, cotangent, codes, scales.reshape(1, OWN))
    keys, gi, gw = pl.pallas_call(
        functools.partial(kernel, 1.0 / total**0.5),
        out_shape=(
            jax.ShapeDtypeStruct((T, KV), BF16),
            jax.ShapeDtypeStruct((T, D), BF16),
            jax.ShapeDtypeStruct((OWN, HALF), F32),
        ),
        in_specs=[hbm] * 4,
        out_specs=(vmem, vmem, vmem),
        scratch_shapes=scratch,
        compiler_params=pltpu.CompilerParams(
            collective_id=0, has_side_effects=True, vmem_limit_bytes=40 << 20
        ),
        name="fused",
    )(*[pltpu.with_memory_space_constraint(a, pltpu.HBM) for a in arrays])
    return pl.pallas_call(
        store,
        out_shape=(
            jax.ShapeDtypeStruct((T, KV), BF16),
            jax.ShapeDtypeStruct((T, D), BF16),
            jax.ShapeDtypeStruct((OWN, HALF), F32),
        ),
        in_specs=[vmem, vmem, vmem],
        out_specs=(hbm, hbm, hbm),
        scratch_shapes=[dma((3,))],
        name="store",
    )(*[pltpu.with_memory_space_constraint(a, pltpu.VMEM) for a in (keys, gi, gw)])


def solution(mesh):
    in_specs = (
        P(("node", "local"), None),
        P(("node", "local"), None),
        P(("node", "local"), None),
        P(("node", "local")),
    )
    out_specs = (P(("node", "local"), None), P(("node", "local"), None), P(("node", "local"), None))
    return jax.shard_map(
        per_device, mesh=mesh, in_specs=in_specs, out_specs=out_specs, check_vma=False
    )
```

```python
import functools

import jax
import jax.numpy as jnp
from jax import lax
from jax.experimental import pallas as pl
from jax.experimental.pallas import tpu as pltpu
from jax.sharding import PartitionSpec as P

NX, NY, NZ = 4, 8, 12
D, KV, T = 4096, 512, 128
HALF = KV // 2
OWN = 11
SLAB = OWN * NY
PLANE = SLAB * NZ
ROWS = PLANE * NX
PAD = ROWS - D
PIECE = 4 * SLAB
CH = 512
NCH = D // CH
MESH = pl.DeviceIdType.MESH
F32, BF16 = jnp.float32, jnp.bfloat16


def mod(a, n):
    return lax.rem(a, n)


def kernel(
    factor,
    tok_hbm, cot_hbm, codes_hbm, scales_hbm, keys, gi, gw,
    tok2, cot2, wpair, stage, chunk, zpack, zbuf, w32,
    part, xr, r32, frag, ysend, ymid, yhalf, yrecv, ysum, zsend, zrecv, fin,
    gi32, gsend, grecv, ksend, krecv, codes, scales,
    lsem, sib_s, sib_r, out, into, tk_r, za_r, zy_r, xs_r, ys_r,
):
    node = lax.axis_index("node")
    local = lax.axis_index("local")
    x = lax.div(node, NZ * 2)
    z = mod(lax.div(node, 2), NZ)
    k = mod(node, 2) * 4 + lax.div(local, 2)
    y = lax.div(local, 2) * 2 + mod(node, 2)
    c = mod(local, 2)
    odd = mod(x + node, 2)

    def dev(x, z, k, c):
        return ((x * NZ + z) * 2 + lax.div(k, 4), mod(k, 4) * 2 + c)

    def at_y(y):
        y = mod(y, NY)
        return dev(x, z, mod(y, 2) * 4 + lax.div(y, 2), c)

    def kof(d):
        to = mod(y + NY + d, NY)
        return mod(to, 2) * 4 + lax.div(to, 2)

    sib = dev(x, z, k, 1 - c)
    xdev = [dev(mod(x + o, NX), z, k, c) for o in range(1, NX)]
    zdev = [dev(x, mod(z + o, NZ), k, c) for o in range(1, NZ)]
    right, left = xdev[0], xdev[2]
    zright, zleft = zdev[0], zdev[NZ - 2]
    up, down = at_y(y + 1), at_y(y + NY - 1)

    def rc(src, dst, ss, rs, to):
        return pltpu.make_async_remote_copy(
            src_ref=src, dst_ref=dst, send_sem=ss, recv_sem=rs, device_id=to, device_id_type=MESH
        )

    def all_sent(stage, ref):
        rc(ref, ref, out.at[stage], into.at[0], sib).wait_send()

    def all_here(sem, ref):
        rc(ref, ref, out.at[0], sem, sib).wait_recv()

    def plane_dev(o):
        return dev(mod(x + lax.div(o, NY), NX), z, mod(k + o, NY), c)

    load_cot = pltpu.make_async_copy(cot_hbm, cot2.at[0:T], lsem.at[1])
    load_tok = pltpu.make_async_copy(tok_hbm, tok2.at[0:T, 0:D], lsem.at[0])
    load_codes = pltpu.make_async_copy(codes_hbm, codes, lsem.at[2])
    load_scales = pltpu.make_async_copy(scales_hbm, scales, lsem.at[3])
    for load in (load_scales, load_codes, load_cot, load_tok):
        load.start()

    barrier = pltpu.get_barrier_semaphore()

    def signal(to):
        pl.semaphore_signal(barrier, inc=1, device_id=to, device_id_type=MESH)

    def signal_plane(o, _):
        signal(plane_dev(o))
        return 0

    def signal_z(o, _):
        signal(dev(x, mod(z + o, NZ), k, c))
        return 0

    signal(sib)
    lax.fori_loop(1, NX * NY, signal_plane, 0)
    lax.fori_loop(1, NZ, signal_z, 0)
    frag[...] = jnp.zeros_like(frag)
    ysum[...] = jnp.zeros_like(ysum)
    tok2[:, D:] = jnp.zeros((2 * T, PAD), BF16)
    stage[...] = jnp.zeros_like(stage)
    load_scales.wait()
    load_codes.wait()
    eye = lax.broadcasted_iota(jnp.int32, (OWN, OWN), 0) == lax.broadcasted_iota(
        jnp.int32, (OWN, OWN), 1
    )
    row = jnp.broadcast_to(scales[...].astype(F32), (OWN, OWN))
    column = jnp.sum(jnp.where(eye, row, 0.0), axis=1, keepdims=True)
    wpair[c, 0:OWN, :] = codes[...].astype(F32) * column
    pl.semaphore_wait(barrier, 1 + NX * NY - 1 + NZ - 1)

    cw = rc(wpair.at[c], wpair.at[c], sib_s.at[0], sib_r.at[0], sib)
    cw.start()
    cc = rc(cot_hbm, cot2.at[T : 2 * T], sib_s.at[1], sib_r.at[1], sib)
    cc.start()

    def quarter(o):
        at = pl.ds(pl.multiple_of(mod(x + o, NX) * 1024, 1024), 1024)
        return rc(
            tok_hbm.at[:, at], tok2.at[T : 2 * T, at], out.at[0], tk_r.at[mod(x + o, NX)], sib
        )

    for o in (2, 3, 0, 1):
        quarter(o).start()
    cw.wait()
    for r in range(OWN):
        rows = []
        for e in range(2):
            i = 2 * r + e
            rows.append(wpair[i // OWN, i % OWN : i % OWN + 1, :])
        stage[r : r + 1, :] = jnp.where(c == 0, rows[0], rows[1])
    me = x * NY + k
    chunk[me] = stage[...].astype(BF16)

    def chunk_copy(o, slot):
        return rc(chunk.at[slot], chunk.at[slot], out.at[1], into.at[0], plane_dev(o))

    def chunk_start(i, _):
        chunk_copy(NX * NY - 1 - i, me).start()
        return 0

    lax.fori_loop(0, NX * NY - 1, chunk_start, 0)

    load_cot.wait()
    load_tok.wait()
    cc.wait()
    mine = pl.ds(pl.multiple_of(c * HALF, 128), HALF)

    def term(p):
        def step(j, _):
            at = pl.multiple_of(p * 1024 + j * 384, 128)
            t = lax.dot_general(
                tok2[:, pl.ds(at, 384)], cot2[:, mine], (((0,), (0,)), ((), ())),
                preferred_element_type=F32,
            )
            t = (t * factor).astype(BF16)
            to = pl.ds(pl.multiple_of(j * 384, 16), 384)
            part[p, 0, to, :] = t[:, :128]
            part[p, 1, to, :] = t[:, 128:]
            return 0

        lax.fori_loop(0, 3, step, 0)

    def piece(p, zz):
        return pl.ds(pl.multiple_of(p * 32 + zz * PIECE, 16), PIECE)

    pr, pf, pl_ = mod(x + 1, NX), mod(x + 2, NX), mod(x + 3, NX)

    def xsum(s, zz):
        p, h, to = [
            (pf, 0, right), (pf, 1, left), (pr, 1, right), (pl_, 0, left), (pr, 0, right), (pl_, 1, left),
        ][s]
        return rc(
            part.at[p, h, piece(p, zz)], xr.at[s, zz], out.at[4], xs_r.at[0 if s < 2 else 1, zz], to
        )

    def far(zz):
        xsum(0, zz).start()
        xsum(1, zz).start()

    def near(zz):
        xsum(2, zz).start()
        xsum(3, zz).start()

    def hand_on(zz):
        all_here(xs_r.at[0, zz], xr.at[0:2, zz])
        for s, h, p in ((0, 0, pr), (1, 1, pl_)):
            rows = piece(p, zz)
            part[p, h, rows, :] = (
                part[p, h, rows, :].astype(F32) + xr[s, zz].astype(F32)
            ).astype(BF16)
            xsum(s + 4, zz).start()

    def root(zz):
        all_here(xs_r.at[1, zz], xr.at[2:6, zz])
        own = piece(x, zz)
        r32[:, 0:128] = part[x, 0, own, :].astype(F32) + (
            xr[3, zz].astype(F32) + xr[4, zz].astype(F32)
        )
        r32[:, 128:256] = part[x, 1, own, :].astype(F32) + (
            xr[2, zz].astype(F32) + xr[5, zz].astype(F32)
        )
        for kk in range(NY):
            for i in range(4):
                at = SLAB * i + OWN * kk
                frag[kk, OWN * i : OWN * (i + 1), :] = r32[at : at + OWN, :]
        for kk in range(NY):
            for h in range(2):
                ysend[zz, kk, h] = frag[kk][:, 128 * h : 128 * h + 128].astype(BF16)
        for n in range(6):
            ysum_copy(zz, n).start()

    def ysum_copy(zz, n):
        row = ysend.at[zz, kof((-3, 3, 4, 4, -1, 1, -2, 2)[n])]
        src, dst, to = [
            (row, ymid.at[zz, 0], -1),
            (row, ymid.at[zz, 1], 1),
            (row.at[0], yhalf.at[zz, 0], -2),
            (row.at[1], yhalf.at[zz, 1], 2),
            (row, yrecv.at[zz, 0], -1),
            (row, yrecv.at[zz, 1], 1),
            (row, yrecv.at[zz, 2], -2),
            (row, yrecv.at[zz, 3], 2),
        ][n]
        return rc(src, dst, out.at[5], ys_r.at[0 if n < 4 else 1, zz], at_y(y + NY + to))

    def mid(zz):
        all_here(ys_r.at[0, zz], ysend.at[zz, 0:3])
        for e in range(2):
            kk = kof((-2, 2)[e])
            for h in range(2):
                t = ysend[zz, kk, h].astype(F32) + ymid[zz, e, h].astype(F32)
                if h == e:
                    t = t + yhalf[zz, e].astype(F32)
                ysend[zz, kk, h] = t.astype(BF16)
            ysum_copy(zz, 6 + e).start()

    def zsum(zz):
        all_here(ys_r.at[1, zz], yrecv.at[zz])
        for h in range(2):
            t = ysend[zz, k, h].astype(F32)
            for e in range(4):
                t = t + yrecv[zz, e, h].astype(F32)
            ysum[0:48, 128 * h : 128 * h + 128] = t
        for i in range(4):
            zt = 4 * zz + i
            zsend[zt] = ysum[OWN * i : OWN * i + 16, :].astype(BF16)

            @pl.when(zt != z)
            def _():
                rc(zsend.at[zt], zrecv.at[z], out.at[6], into.at[1], dev(x, zt, k, c)).start()

            @pl.when(zt == z)
            def _():
                zrecv[zt] = zsend[zt]

    quarter(2).wait_recv()
    quarter(3).wait_recv()
    term(pf)
    far(0)
    quarter(0).wait_recv()
    term(pl_)
    quarter(1).wait_recv()
    term(pr)
    near(0)
    far(1)
    term(x)
    hand_on(0)
    far(2)
    near(1)

    all_here(into.at[0], chunk.at[0 : NX * NY - 1])
    for q in range(2):
        for e in range(2):
            for j in range(NY):
                at = SLAB * e + OWN * j
                zpack[at : at + OWN, :] = chunk[(2 * q + e) * NY + j].astype(F32)[:OWN]
        for h in range(2):
            zbuf[z, q, h] = zpack[:, 128 * h : 128 * h + 128].astype(BF16)

    def zslot(way, t):
        return mod(z + (NZ - t if way == 0 else t), NZ)

    def zhalves(way, t):
        return (0, 1) if t < 6 else (way,)

    def zcopy(way, t, h):
        at = zslot(way, t - 1)
        return rc(
            zbuf.at[at, odd, h], zbuf.at[at, odd, h], out.at[2], za_r.at[at, h],
            zright if way == 0 else zleft,
        )

    def zarrived(way, t, h):
        at = zslot(way, t)
        rc(
            zbuf.at[at, odd, h], zbuf.at[at, odd, h], out.at[2], za_r.at[at, h],
            zright if way == 0 else zleft,
        ).wait_recv()

    def across(way, t, h, q):
        at = zslot(way, t)
        return rc(
            zbuf.at[at, q, h], zbuf.at[at, q, h], out.at[3], zy_r.at[t - 1],
            (up, down, right, left)[h if t < 4 else 2 + h],
        )

    def place(at, q, h):
        v = zbuf[at, q, h].astype(F32)
        for e in range(2):
            to = pl.multiple_of((2 * q + e) * PLANE + at * SLAB, 8)
            w32[pl.ds(to, SLAB), 128 * h : 128 * h + 128] = v[e * SLAB : (e + 1) * SLAB]

    def zstep(t):
        for h in range(2):
            for way in range(2):
                if h not in zhalves(way, t):
                    continue
                zarrived(way, t, h)
                if t < 6 and h in zhalves(way, t + 1):
                    zcopy(way, t + 1, h).start()
                across(way, t, h, odd).start()
        for h in range(2):
            for way in range(2):
                if h in zhalves(way, t):
                    place(zslot(way, t), odd, h)

    def from_side(t):
        all_here(zy_r.at[t - 1], zbuf.at[0:2, 0] if t < 6 else zbuf.at[0, 0])
        for h in range(2):
            for way in range(2):
                if h in zhalves(way, t):
                    place(zslot(way, t), 1 - odd, h)

    for h in range(2):
        for way in range(2):
            zcopy(way, 1, h).start()
    for q in range(2):
        for h in range(2):
            place(z, q, h)
    hand_on(1)
    near(2)
    zstep(1)
    root(0)
    hand_on(2)
    zstep(2)
    mid(0)
    root(1)
    zstep(3)
    from_side(1)
    zsum(0)
    zstep(4)
    mid(1)
    root(2)
    from_side(2)
    zstep(5)
    zsum(1)
    mid(2)
    from_side(3)
    zstep(6)
    from_side(4)

    def order(j):
        return jnp.where(odd == 0, j, NCH - 1 - j)

    def out_step(i, acc):
        j = order(i)
        at = pl.multiple_of(j * CH, CH)
        w = w32[pl.ds(at, CH), :].astype(BF16)
        acc = acc + jnp.dot(tok2[:, pl.ds(at, CH)], w, preferred_element_type=F32)
        g = lax.dot_general(cot2[:, mine], w, (((1,), (1,)), ((), ())), preferred_element_type=F32)
        gi32[j] = g[:T]
        gsend[j] = g[T:].astype(BF16)
        rc(gsend.at[j], grecv.at[j], out.at[7], sib_r.at[5 + j], sib).start()
        return acc

    def join(i):
        j = order(i)
        rc(gsend.at[j], grecv.at[j], out.at[7], sib_r.at[5 + j], sib).wait_recv()
        at = pl.multiple_of(j * CH, CH)
        gi[:, pl.ds(at, CH)] = (gi32[j] + grecv[j].astype(F32)).astype(BF16)

    def out_join(i, acc):
        acc = out_step(i, acc)
        join(i - 3)
        return acc

    acc = lax.fori_loop(0, 3, out_step, jnp.zeros((2 * T, HALF), F32))
    zsum(2)
    from_side(5)
    from_side(6)
    acc = lax.fori_loop(3, NCH, out_join, acc)
    other = pl.ds(pl.multiple_of((1 - c) * HALF, 128), HALF)
    keys[:, mine] = acc[:T].astype(BF16)
    ksend[...] = acc[T:].astype(BF16)
    ck = rc(ksend, krecv, sib_s.at[3], sib_r.at[3], sib)
    ck.start()
    for i in range(NCH - 3, NCH):
        join(i)
    ck.wait()
    keys[:, other] = krecv[...]

    all_here(into.at[1], zrecv.at[0 : NZ - 1])
    s = zrecv[0].astype(F32)
    for j in range(1, NZ):
        s = s + zrecv[j].astype(F32)
    fin[c] = s
    cf = rc(fin.at[c], fin.at[c], sib_s.at[4], sib_r.at[4], sib)
    cf.start()

    all_sent(0, tok2.at[0:T, 0:D])
    all_sent(1, chunk.at[0 : NX * NY - 1])
    all_sent(2, zbuf.at[0:11, 0])
    all_sent(3, zbuf.at[0:11, 0])
    all_sent(4, xr)
    all_sent(5, ysend.at[:, 0:7])
    all_sent(6, zsend.at[0 : NZ - 1])
    all_sent(7, gsend)
    cf.wait()
    for r in range(OWN):
        rows = []
        for e in range(2):
            i = OWN * e + r
            rows.append(fin[i % 2, i // 2 : i // 2 + 1, :])
        gw[r : r + 1, :] = jnp.where(c == 0, rows[0], rows[1])


def store(keys, gi, gw, keys_out, gi_out, gw_out, sem):
    copies = [
        pltpu.make_async_copy(gi, gi_out, sem.at[0]),
        pltpu.make_async_copy(keys, keys_out, sem.at[1]),
        pltpu.make_async_copy(gw, gw_out, sem.at[2]),
    ]
    for copy in copies:
        copy.start()
    for copy in copies:
        copy.wait()


def per_device(tokens, cotangent, codes, scales):
    total = tokens.shape[0] * lax.axis_size("node") * lax.axis_size("local")
    dma = pltpu.SemaphoreType.DMA
    scratch = [
        pltpu.VMEM((2 * T, ROWS), BF16),
        pltpu.VMEM((2 * T, KV), BF16),
        pltpu.VMEM((2, 16, HALF), F32),
        pltpu.VMEM((16, HALF), F32),
        pltpu.VMEM((NX * NY, 16, HALF), BF16),
        pltpu.VMEM((2 * SLAB, HALF), F32),
        pltpu.VMEM((NZ, 2, 2, 2 * SLAB, 128), BF16),
        pltpu.VMEM((ROWS, HALF), F32),
        pltpu.VMEM((NX, 2, 1152, 128), BF16),
        pltpu.VMEM((6, 3, PIECE, 128), BF16),
        pltpu.VMEM((PIECE, HALF), F32),
        pltpu.VMEM((NY, 48, HALF), F32),
        pltpu.VMEM((3, NY, 2, 48, 128), BF16),
        pltpu.VMEM((3, 2, 2, 48, 128), BF16),
        pltpu.VMEM((3, 2, 48, 128), BF16),
        pltpu.VMEM((3, 4, 2, 48, 128), BF16),
        pltpu.VMEM((56, HALF), F32),
        pltpu.VMEM((NZ, 16, HALF), BF16),
        pltpu.VMEM((NZ, 16, HALF), BF16),
        pltpu.VMEM((2, 16, HALF), F32),
        pltpu.VMEM((NCH, T, CH), F32),
        pltpu.VMEM((NCH, T, CH), BF16),
        pltpu.VMEM((NCH, T, CH), BF16),
        pltpu.VMEM((T, HALF), BF16),
        pltpu.VMEM((T, HALF), BF16),
        pltpu.VMEM((OWN, HALF), BF16),
        pltpu.VMEM((1, OWN), BF16),
        dma((4,)),
        dma((5,)), dma((5 + NCH,)),
        dma((8,)), dma((2,)), dma((NX,)),
        dma((NZ, 2)), dma((6,)), dma((2, 3)), dma((2, 3)),
    ]
    vmem = pl.BlockSpec(memory_space=pltpu.VMEM)
    hbm = pl.BlockSpec(memory_space=pl.ANY)
    arrays = (tokens, cotangent, codes, scales.reshape(1, OWN))
    keys, gi, gw = pl.pallas_call(
        functools.partial(kernel, 1.0 / total**0.5),
        out_shape=(
            jax.ShapeDtypeStruct((T, KV), BF16),
            jax.ShapeDtypeStruct((T, D), BF16),
            jax.ShapeDtypeStruct((OWN, HALF), F32),
        ),
        in_specs=[hbm] * 4,
        out_specs=(vmem, vmem, vmem),
        scratch_shapes=scratch,
        compiler_params=pltpu.CompilerParams(
            collective_id=0, has_side_effects=True, vmem_limit_bytes=40 << 20
        ),
        name="fused",
    )(*[pltpu.with_memory_space_constraint(a, pltpu.HBM) for a in arrays])
    return pl.pallas_call(
        store,
        out_shape=(
            jax.ShapeDtypeStruct((T, KV), BF16),
            jax.ShapeDtypeStruct((T, D), BF16),
            jax.ShapeDtypeStruct((OWN, HALF), F32),
        ),
        in_specs=[vmem, vmem, vmem],
        out_specs=(hbm, hbm, hbm),
        scratch_shapes=[dma((3,))],
        name="store",
    )(*[pltpu.with_memory_space_constraint(a, pltpu.VMEM) for a in (keys, gi, gw)])


def solution(mesh):
    in_specs = (
        P(("node", "local"), None),
        P(("node", "local"), None),
        P(("node", "local"), None),
        P(("node", "local")),
    )
    out_specs = (P(("node", "local"), None), P(("node", "local"), None), P(("node", "local"), None))
    return jax.shard_map(
        per_device, mesh=mesh, in_specs=in_specs, out_specs=out_specs, check_vma=False
    )
```

```python
import functools

import jax
import jax.numpy as jnp
from jax import lax
from jax.experimental import pallas as pl
from jax.experimental.pallas import tpu as pltpu
from jax.sharding import PartitionSpec as P

NX, NY, NZ = 4, 8, 12
D, KV, T = 4096, 512, 128
HALF = KV // 2
OWN = 11
SLAB = OWN * NY
PLANE = SLAB * NZ
ROWS = PLANE * NX
PAD = ROWS - D
PIECE = 4 * SLAB
CH = 512
NCH = D // CH
MESH = pl.DeviceIdType.MESH
F32, BF16 = jnp.float32, jnp.bfloat16


def mod(a, n):
    return lax.rem(a, n)


def kernel(
    factor,
    tok_hbm, cot_hbm, codes_hbm, scales_hbm, keys, gi, gw,
    tok2, cot2, wpair, stage, chunk, zpack, zbuf, w32,
    part, xr, r32, frag, ysend, ymid, yhalf, yrecv, ysum, zsend, zrecv, fin,
    gi32, gsend, grecv, ksend, krecv, codes, scales,
    lsem, sib_s, sib_r, out, into, tk_r, za_r, zy_r, xs_r, ys_r,
):
    node = lax.axis_index("node")
    local = lax.axis_index("local")
    x = lax.div(node, NZ * 2)
    z = mod(lax.div(node, 2), NZ)
    k = mod(node, 2) * 4 + lax.div(local, 2)
    y = lax.div(local, 2) * 2 + mod(node, 2)
    c = mod(local, 2)
    odd = mod(x + node, 2)

    def dev(x, z, k, c):
        return ((x * NZ + z) * 2 + lax.div(k, 4), mod(k, 4) * 2 + c)

    def at_y(y):
        y = mod(y, NY)
        return dev(x, z, mod(y, 2) * 4 + lax.div(y, 2), c)

    def kof(d):
        to = mod(y + NY + d, NY)
        return mod(to, 2) * 4 + lax.div(to, 2)

    sib = dev(x, z, k, 1 - c)
    xdev = [dev(mod(x + o, NX), z, k, c) for o in range(1, NX)]
    zdev = [dev(x, mod(z + o, NZ), k, c) for o in range(1, NZ)]
    right, left = xdev[0], xdev[2]
    zright, zleft = zdev[0], zdev[NZ - 2]
    up, down = at_y(y + 1), at_y(y + NY - 1)

    def rc(src, dst, ss, rs, to):
        return pltpu.make_async_remote_copy(
            src_ref=src, dst_ref=dst, send_sem=ss, recv_sem=rs, device_id=to, device_id_type=MESH
        )

    def all_sent(stage, ref):
        rc(ref, ref, out.at[stage], into.at[0], sib).wait_send()

    def all_here(sem, ref):
        rc(ref, ref, out.at[0], sem, sib).wait_recv()

    def plane_dev(o):
        return dev(mod(x + lax.div(o, NY), NX), z, mod(k + o, NY), c)

    load_cot = pltpu.make_async_copy(cot_hbm, cot2.at[0:T], lsem.at[1])
    load_tok = pltpu.make_async_copy(tok_hbm, tok2.at[0:T, 0:D], lsem.at[0])
    load_codes = pltpu.make_async_copy(codes_hbm, codes, lsem.at[2])
    load_scales = pltpu.make_async_copy(scales_hbm, scales, lsem.at[3])
    for load in (load_scales, load_codes, load_cot, load_tok):
        load.start()

    barrier = pltpu.get_barrier_semaphore()

    def signal(to):
        pl.semaphore_signal(barrier, inc=1, device_id=to, device_id_type=MESH)

    def signal_plane(o, _):
        signal(plane_dev(o))
        return 0

    def signal_z(o, _):
        signal(dev(x, mod(z + o, NZ), k, c))
        return 0

    signal(sib)
    lax.fori_loop(1, NX * NY, signal_plane, 0)
    lax.fori_loop(1, NZ, signal_z, 0)
    frag[...] = jnp.zeros_like(frag)
    ysum[...] = jnp.zeros_like(ysum)
    tok2[:, D:] = jnp.zeros((2 * T, PAD), BF16)
    stage[...] = jnp.zeros_like(stage)
    load_scales.wait()
    load_codes.wait()
    eye = lax.broadcasted_iota(jnp.int32, (OWN, OWN), 0) == lax.broadcasted_iota(
        jnp.int32, (OWN, OWN), 1
    )
    row = jnp.broadcast_to(scales[...].astype(F32), (OWN, OWN))
    column = jnp.sum(jnp.where(eye, row, 0.0), axis=1, keepdims=True)
    wpair[c, 0:OWN, :] = codes[...].astype(F32) * column
    pl.semaphore_wait(barrier, 1 + NX * NY - 1 + NZ - 1)

    cw = rc(wpair.at[c], wpair.at[c], sib_s.at[0], sib_r.at[0], sib)
    cw.start()
    cc = rc(cot_hbm, cot2.at[T : 2 * T], sib_s.at[1], sib_r.at[1], sib)
    cc.start()

    def quarter(o):
        at = pl.ds(pl.multiple_of(mod(x + o, NX) * 1024, 1024), 1024)
        return rc(
            tok_hbm.at[:, at], tok2.at[T : 2 * T, at], out.at[0], tk_r.at[mod(x + o, NX)], sib
        )

    for o in (2, 3, 0, 1):
        quarter(o).start()
    cw.wait()
    for r in range(OWN):
        rows = []
        for e in range(2):
            i = 2 * r + e
            rows.append(wpair[i // OWN, i % OWN : i % OWN + 1, :])
        stage[r : r + 1, :] = jnp.where(c == 0, rows[0], rows[1])
    me = x * NY + k
    chunk[me] = stage[...].astype(BF16)

    def chunk_copy(o, slot):
        return rc(chunk.at[slot], chunk.at[slot], out.at[1], into.at[0], plane_dev(o))

    def chunk_start(i, _):
        chunk_copy(NX * NY - 1 - i, me).start()
        return 0

    lax.fori_loop(0, NX * NY - 1, chunk_start, 0)

    load_cot.wait()
    load_tok.wait()
    cc.wait()
    mine = pl.ds(pl.multiple_of(c * HALF, 128), HALF)

    def term(p):
        def step(j, _):
            at = pl.multiple_of(p * 1024 + j * 384, 128)
            t = lax.dot_general(
                tok2[:, pl.ds(at, 384)], cot2[:, mine], (((0,), (0,)), ((), ())),
                preferred_element_type=F32,
            )
            t = (t * factor).astype(BF16)
            to = pl.ds(pl.multiple_of(j * 384, 16), 384)
            part[p, 0, to, :] = t[:, :128]
            part[p, 1, to, :] = t[:, 128:]
            return 0

        lax.fori_loop(0, 3, step, 0)

    def piece(p, zz):
        return pl.ds(pl.multiple_of(p * 32 + zz * PIECE, 16), PIECE)

    pr, pf, pl_ = mod(x + 1, NX), mod(x + 2, NX), mod(x + 3, NX)

    def xsum(s, zz):
        p, h, to = [
            (pf, 0, right), (pf, 1, left), (pr, 1, right), (pl_, 0, left), (pr, 0, right), (pl_, 1, left),
        ][s]
        return rc(
            part.at[p, h, piece(p, zz)], xr.at[s, zz], out.at[4], xs_r.at[0 if s < 2 else 1, zz], to
        )

    def far(zz):
        xsum(0, zz).start()
        xsum(1, zz).start()

    def near(zz):
        xsum(2, zz).start()
        xsum(3, zz).start()

    def hand_on(zz):
        all_here(xs_r.at[0, zz], xr.at[0:2, zz])
        for s, h, p in ((0, 0, pr), (1, 1, pl_)):
            rows = piece(p, zz)
            part[p, h, rows, :] = (
                part[p, h, rows, :].astype(F32) + xr[s, zz].astype(F32)
            ).astype(BF16)
            xsum(s + 4, zz).start()

    def root(zz):
        all_here(xs_r.at[1, zz], xr.at[2:6, zz])
        own = piece(x, zz)
        r32[:, 0:128] = part[x, 0, own, :].astype(F32) + (
            xr[3, zz].astype(F32) + xr[4, zz].astype(F32)
        )
        r32[:, 128:256] = part[x, 1, own, :].astype(F32) + (
            xr[2, zz].astype(F32) + xr[5, zz].astype(F32)
        )
        for kk in range(NY):
            for i in range(4):
                at = SLAB * i + OWN * kk
                frag[kk, OWN * i : OWN * (i + 1), :] = r32[at : at + OWN, :]
        for kk in range(NY):
            for h in range(2):
                ysend[zz, kk, h] = frag[kk][:, 128 * h : 128 * h + 128].astype(BF16)
        for n in range(6):
            ysum_copy(zz, n).start()

    def ysum_copy(zz, n):
        row = ysend.at[zz, kof((-3, 3, 4, 4, -1, 1, -2, 2)[n])]
        src, dst, to = [
            (row, ymid.at[zz, 0], -1),
            (row, ymid.at[zz, 1], 1),
            (row.at[0], yhalf.at[zz, 0], -2),
            (row.at[1], yhalf.at[zz, 1], 2),
            (row, yrecv.at[zz, 0], -1),
            (row, yrecv.at[zz, 1], 1),
            (row, yrecv.at[zz, 2], -2),
            (row, yrecv.at[zz, 3], 2),
        ][n]
        return rc(src, dst, out.at[5], ys_r.at[0 if n < 4 else 1, zz], at_y(y + NY + to))

    def mid(zz):
        all_here(ys_r.at[0, zz], ysend.at[zz, 0:3])
        for e in range(2):
            kk = kof((-2, 2)[e])
            for h in range(2):
                t = ysend[zz, kk, h].astype(F32) + ymid[zz, e, h].astype(F32)
                if h == e:
                    t = t + yhalf[zz, e].astype(F32)
                ysend[zz, kk, h] = t.astype(BF16)
            ysum_copy(zz, 6 + e).start()

    def zsum(zz):
        all_here(ys_r.at[1, zz], yrecv.at[zz])
        for h in range(2):
            t = ysend[zz, k, h].astype(F32)
            for e in range(4):
                t = t + yrecv[zz, e, h].astype(F32)
            ysum[0:48, 128 * h : 128 * h + 128] = t
        for i in range(4):
            zt = 4 * zz + i
            zsend[zt] = ysum[OWN * i : OWN * i + 16, :].astype(BF16)

            @pl.when(zt != z)
            def _():
                rc(zsend.at[zt], zrecv.at[z], out.at[6], into.at[1], dev(x, zt, k, c)).start()

            @pl.when(zt == z)
            def _():
                zrecv[zt] = zsend[zt]

    quarter(2).wait_recv()
    quarter(3).wait_recv()
    term(pf)
    far(0)
    quarter(0).wait_recv()
    term(pl_)
    quarter(1).wait_recv()
    term(pr)
    near(0)
    far(1)
    term(x)
    hand_on(0)
    far(2)
    near(1)

    all_here(into.at[0], chunk.at[0 : NX * NY - 1])
    for q in range(2):
        for e in range(2):
            for j in range(NY):
                at = SLAB * e + OWN * j
                zpack[at : at + OWN, :] = chunk[(2 * q + e) * NY + j].astype(F32)[:OWN]
        for h in range(2):
            zbuf[z, q, h] = zpack[:, 128 * h : 128 * h + 128].astype(BF16)

    def zslot(way, t):
        return mod(z + (NZ - t if way == 0 else t), NZ)

    def zhalves(way, t):
        return (0, 1) if t < 6 else (way,)

    def zcopy(way, t, h):
        at = zslot(way, t - 1)
        return rc(
            zbuf.at[at, odd, h], zbuf.at[at, odd, h], out.at[2], za_r.at[at, h],
            zright if way == 0 else zleft,
        )

    def zarrived(way, t, h):
        at = zslot(way, t)
        rc(
            zbuf.at[at, odd, h], zbuf.at[at, odd, h], out.at[2], za_r.at[at, h],
            zright if way == 0 else zleft,
        ).wait_recv()

    def across(way, t, h, q):
        at = zslot(way, t)
        return rc(
            zbuf.at[at, q, h], zbuf.at[at, q, h], out.at[3], zy_r.at[t - 1],
            (up, down, right, left)[h if t < 4 else 2 + h],
        )

    def place(at, q, h):
        v = zbuf[at, q, h].astype(F32)
        for e in range(2):
            to = pl.multiple_of((2 * q + e) * PLANE + at * SLAB, 8)
            w32[pl.ds(to, SLAB), 128 * h : 128 * h + 128] = v[e * SLAB : (e + 1) * SLAB]

    def zstep(t):
        for h in range(2):
            for way in range(2):
                if h not in zhalves(way, t):
                    continue
                zarrived(way, t, h)
                if t < 6 and h in zhalves(way, t + 1):
                    zcopy(way, t + 1, h).start()
                across(way, t, h, odd).start()
        for h in range(2):
            for way in range(2):
                if h in zhalves(way, t):
                    place(zslot(way, t), odd, h)

    def from_side(t):
        all_here(zy_r.at[t - 1], zbuf.at[0:2, 0] if t < 6 else zbuf.at[0, 0])
        for h in range(2):
            for way in range(2):
                if h in zhalves(way, t):
                    place(zslot(way, t), 1 - odd, h)

    for h in range(2):
        for way in range(2):
            zcopy(way, 1, h).start()
    for q in range(2):
        for h in range(2):
            place(z, q, h)
    zstep(1)
    hand_on(1)
    near(2)
    root(0)
    zstep(2)
    hand_on(2)
    zstep(3)
    mid(0)
    root(1)
    zstep(4)
    from_side(1)
    zsum(0)
    root(2)
    mid(1)
    zstep(5)
    from_side(2)
    from_side(3)
    mid(2)
    zsum(1)
    zstep(6)
    from_side(4)

    def order(j):
        return jnp.where(odd == 0, j, NCH - 1 - j)

    def out_step(i, acc):
        j = order(i)
        at = pl.multiple_of(j * CH, CH)
        w = w32[pl.ds(at, CH), :].astype(BF16)
        acc = acc + jnp.dot(tok2[:, pl.ds(at, CH)], w, preferred_element_type=F32)
        g = lax.dot_general(cot2[:, mine], w, (((1,), (1,)), ((), ())), preferred_element_type=F32)
        gi32[j] = g[:T]
        gsend[j] = g[T:].astype(BF16)
        rc(gsend.at[j], grecv.at[j], out.at[7], sib_r.at[5 + j], sib).start()
        return acc

    def join(i):
        j = order(i)
        rc(gsend.at[j], grecv.at[j], out.at[7], sib_r.at[5 + j], sib).wait_recv()
        at = pl.multiple_of(j * CH, CH)
        gi[:, pl.ds(at, CH)] = (gi32[j] + grecv[j].astype(F32)).astype(BF16)

    acc = lax.fori_loop(0, 3, out_step, jnp.zeros((2 * T, HALF), F32))
    from_side(5)
    zsum(2)
    from_side(6)
    acc = lax.fori_loop(3, NCH, out_step, acc)
    other = pl.ds(pl.multiple_of((1 - c) * HALF, 128), HALF)
    keys[:, mine] = acc[:T].astype(BF16)
    ksend[...] = acc[T:].astype(BF16)
    ck = rc(ksend, krecv, sib_s.at[3], sib_r.at[3], sib)
    ck.start()
    for i in range(NCH):
        join(i)
    ck.wait()
    keys[:, other] = krecv[...]

    all_here(into.at[1], zrecv.at[0 : NZ - 1])
    s = zrecv[0].astype(F32)
    for j in range(1, NZ):
        s = s + zrecv[j].astype(F32)
    fin[c] = s
    cf = rc(fin.at[c], fin.at[c], sib_s.at[4], sib_r.at[4], sib)
    cf.start()

    all_sent(0, tok2.at[0:T, 0:D])
    all_sent(1, chunk.at[0 : NX * NY - 1])
    all_sent(2, zbuf.at[0:11, 0])
    all_sent(3, zbuf.at[0:11, 0])
    all_sent(4, xr)
    all_sent(5, ysend.at[:, 0:7])
    all_sent(6, zsend.at[0 : NZ - 1])
    all_sent(7, gsend)
    cf.wait()
    for r in range(OWN):
        rows = []
        for e in range(2):
            i = OWN * e + r
            rows.append(fin[i % 2, i // 2 : i // 2 + 1, :])
        gw[r : r + 1, :] = jnp.where(c == 0, rows[0], rows[1])


def store(keys, gi, gw, keys_out, gi_out, gw_out, sem):
    copies = [
        pltpu.make_async_copy(gi, gi_out, sem.at[0]),
        pltpu.make_async_copy(keys, keys_out, sem.at[1]),
        pltpu.make_async_copy(gw, gw_out, sem.at[2]),
    ]
    for copy in copies:
        copy.start()
    for copy in copies:
        copy.wait()


def per_device(tokens, cotangent, codes, scales):
    total = tokens.shape[0] * lax.axis_size("node") * lax.axis_size("local")
    dma = pltpu.SemaphoreType.DMA
    scratch = [
        pltpu.VMEM((2 * T, ROWS), BF16),
        pltpu.VMEM((2 * T, KV), BF16),
        pltpu.VMEM((2, 16, HALF), F32),
        pltpu.VMEM((16, HALF), F32),
        pltpu.VMEM((NX * NY, 16, HALF), BF16),
        pltpu.VMEM((2 * SLAB, HALF), F32),
        pltpu.VMEM((NZ, 2, 2, 2 * SLAB, 128), BF16),
        pltpu.VMEM((ROWS, HALF), F32),
        pltpu.VMEM((NX, 2, 1152, 128), BF16),
        pltpu.VMEM((6, 3, PIECE, 128), BF16),
        pltpu.VMEM((PIECE, HALF), F32),
        pltpu.VMEM((NY, 48, HALF), F32),
        pltpu.VMEM((3, NY, 2, 48, 128), BF16),
        pltpu.VMEM((3, 2, 2, 48, 128), BF16),
        pltpu.VMEM((3, 2, 48, 128), BF16),
        pltpu.VMEM((3, 4, 2, 48, 128), BF16),
        pltpu.VMEM((56, HALF), F32),
        pltpu.VMEM((NZ, 16, HALF), BF16),
        pltpu.VMEM((NZ, 16, HALF), BF16),
        pltpu.VMEM((2, 16, HALF), F32),
        pltpu.VMEM((NCH, T, CH), F32),
        pltpu.VMEM((NCH, T, CH), BF16),
        pltpu.VMEM((NCH, T, CH), BF16),
        pltpu.VMEM((T, HALF), BF16),
        pltpu.VMEM((T, HALF), BF16),
        pltpu.VMEM((OWN, HALF), BF16),
        pltpu.VMEM((1, OWN), BF16),
        dma((4,)),
        dma((5,)), dma((5 + NCH,)),
        dma((8,)), dma((2,)), dma((NX,)),
        dma((NZ, 2)), dma((6,)), dma((2, 3)), dma((2, 3)),
    ]
    vmem = pl.BlockSpec(memory_space=pltpu.VMEM)
    hbm = pl.BlockSpec(memory_space=pl.ANY)
    arrays = (tokens, cotangent, codes, scales.reshape(1, OWN))
    keys, gi, gw = pl.pallas_call(
        functools.partial(kernel, 1.0 / total**0.5),
        out_shape=(
            jax.ShapeDtypeStruct((T, KV), BF16),
            jax.ShapeDtypeStruct((T, D), BF16),
            jax.ShapeDtypeStruct((OWN, HALF), F32),
        ),
        in_specs=[hbm] * 4,
        out_specs=(vmem, vmem, vmem),
        scratch_shapes=scratch,
        compiler_params=pltpu.CompilerParams(
            collective_id=0, has_side_effects=True, vmem_limit_bytes=40 << 20
        ),
        name="fused",
    )(*[pltpu.with_memory_space_constraint(a, pltpu.HBM) for a in arrays])
    return pl.pallas_call(
        store,
        out_shape=(
            jax.ShapeDtypeStruct((T, KV), BF16),
            jax.ShapeDtypeStruct((T, D), BF16),
            jax.ShapeDtypeStruct((OWN, HALF), F32),
        ),
        in_specs=[vmem, vmem, vmem],
        out_specs=(hbm, hbm, hbm),
        scratch_shapes=[dma((3,))],
        name="store",
    )(*[pltpu.with_memory_space_constraint(a, pltpu.VMEM) for a in (keys, gi, gw)])


def solution(mesh):
    in_specs = (
        P(("node", "local"), None),
        P(("node", "local"), None),
        P(("node", "local"), None),
        P(("node", "local")),
    )
    out_specs = (P(("node", "local"), None), P(("node", "local"), None), P(("node", "local"), None))
    return jax.shard_map(
        per_device, mesh=mesh, in_specs=in_specs, out_specs=out_specs, check_vma=False
    )
```

```python
import functools

import jax
import jax.numpy as jnp
from jax import lax
from jax.experimental import pallas as pl
from jax.experimental.pallas import tpu as pltpu
from jax.sharding import PartitionSpec as P

NX, NY, NZ = 4, 8, 12
D, KV, T = 4096, 512, 128
HALF = KV // 2
OWN = 11
SLAB = OWN * NY
PLANE = SLAB * NZ
ROWS = PLANE * NX
PAD = ROWS - D
PIECE = 4 * SLAB
CH = 512
NCH = D // CH
MESH = pl.DeviceIdType.MESH
F32, BF16 = jnp.float32, jnp.bfloat16


def mod(a, n):
    return lax.rem(a, n)


def kernel(
    factor,
    tok_hbm, cot_hbm, codes_hbm, scales_hbm, keys, gi, gw,
    tok2, cot2, wpair, stage, chunk, zpack, zbuf, w32,
    part, xr, r32, frag, ysend, ymid, yhalf, yrecv, ysum, zsend, zrecv, fin,
    gi32, gsend, grecv, ksend, krecv, codes, scales,
    lsem, sib_s, sib_r, out, into, tk_r, za_r, zy_r, xs_r, ys_r,
):
    node = lax.axis_index("node")
    local = lax.axis_index("local")
    x = lax.div(node, NZ * 2)
    z = mod(lax.div(node, 2), NZ)
    k = mod(node, 2) * 4 + lax.div(local, 2)
    y = lax.div(local, 2) * 2 + mod(node, 2)
    c = mod(local, 2)
    odd = mod(x + node, 2)

    def dev(x, z, k, c):
        return ((x * NZ + z) * 2 + lax.div(k, 4), mod(k, 4) * 2 + c)

    def at_y(y):
        y = mod(y, NY)
        return dev(x, z, mod(y, 2) * 4 + lax.div(y, 2), c)

    def kof(d):
        to = mod(y + NY + d, NY)
        return mod(to, 2) * 4 + lax.div(to, 2)

    sib = dev(x, z, k, 1 - c)
    xdev = [dev(mod(x + o, NX), z, k, c) for o in range(1, NX)]
    zdev = [dev(x, mod(z + o, NZ), k, c) for o in range(1, NZ)]
    right, left = xdev[0], xdev[2]
    zright, zleft = zdev[0], zdev[NZ - 2]
    up, down = at_y(y + 1), at_y(y + NY - 1)

    def rc(src, dst, ss, rs, to):
        return pltpu.make_async_remote_copy(
            src_ref=src, dst_ref=dst, send_sem=ss, recv_sem=rs, device_id=to, device_id_type=MESH
        )

    def all_sent(stage, ref):
        rc(ref, ref, out.at[stage], into.at[0], sib).wait_send()

    def all_here(sem, ref):
        rc(ref, ref, out.at[0], sem, sib).wait_recv()

    def plane_dev(o):
        return dev(mod(x + lax.div(o, NY), NX), z, mod(k + o, NY), c)

    load_cot = pltpu.make_async_copy(cot_hbm, cot2.at[0:T], lsem.at[1])
    load_tok = pltpu.make_async_copy(tok_hbm, tok2.at[0:T, 0:D], lsem.at[0])
    load_codes = pltpu.make_async_copy(codes_hbm, codes, lsem.at[2])
    load_scales = pltpu.make_async_copy(scales_hbm, scales, lsem.at[3])
    for load in (load_scales, load_codes, load_cot, load_tok):
        load.start()

    barrier = pltpu.get_barrier_semaphore()

    def signal(to):
        pl.semaphore_signal(barrier, inc=1, device_id=to, device_id_type=MESH)

    def signal_plane(o, _):
        signal(plane_dev(o))
        return 0

    def signal_z(o, _):
        signal(dev(x, mod(z + o, NZ), k, c))
        return 0

    signal(sib)
    lax.fori_loop(1, NX * NY, signal_plane, 0)
    lax.fori_loop(1, NZ, signal_z, 0)
    frag[...] = jnp.zeros_like(frag)
    ysum[...] = jnp.zeros_like(ysum)
    tok2[:, D:] = jnp.zeros((2 * T, PAD), BF16)
    stage[...] = jnp.zeros_like(stage)
    load_scales.wait()
    load_codes.wait()
    eye = lax.broadcasted_iota(jnp.int32, (OWN, OWN), 0) == lax.broadcasted_iota(
        jnp.int32, (OWN, OWN), 1
    )
    row = jnp.broadcast_to(scales[...].astype(F32), (OWN, OWN))
    column = jnp.sum(jnp.where(eye, row, 0.0), axis=1, keepdims=True)
    wpair[c, 0:OWN, :] = codes[...].astype(F32) * column
    pl.semaphore_wait(barrier, 1 + NX * NY - 1 + NZ - 1)

    cw = rc(wpair.at[c], wpair.at[c], sib_s.at[0], sib_r.at[0], sib)
    cw.start()
    cc = rc(cot_hbm, cot2.at[T : 2 * T], sib_s.at[1], sib_r.at[1], sib)
    cc.start()

    def quarter(o):
        at = pl.ds(pl.multiple_of(mod(x + o, NX) * 1024, 1024), 1024)
        return rc(
            tok_hbm.at[:, at], tok2.at[T : 2 * T, at], out.at[0], tk_r.at[mod(x + o, NX)], sib
        )

    for o in (2, 3, 0, 1):
        quarter(o).start()
    cw.wait()
    for r in range(OWN):
        rows = []
        for e in range(2):
            i = 2 * r + e
            rows.append(wpair[i // OWN, i % OWN : i % OWN + 1, :])
        stage[r : r + 1, :] = jnp.where(c == 0, rows[0], rows[1])
    me = x * NY + k
    chunk[me] = stage[...].astype(BF16)

    def chunk_copy(o, slot):
        return rc(chunk.at[slot], chunk.at[slot], out.at[1], into.at[0], plane_dev(o))

    def chunk_start(i, _):
        chunk_copy(NX * NY - 1 - i, me).start()
        return 0

    lax.fori_loop(0, NX * NY - 1, chunk_start, 0)

    load_cot.wait()
    load_tok.wait()
    cc.wait()
    mine = pl.ds(pl.multiple_of(c * HALF, 128), HALF)

    def term(p):
        def step(j, _):
            at = pl.multiple_of(p * 1024 + j * 384, 128)
            t = lax.dot_general(
                tok2[:, pl.ds(at, 384)], cot2[:, mine], (((0,), (0,)), ((), ())),
                preferred_element_type=F32,
            )
            t = (t * factor).astype(BF16)
            to = pl.ds(pl.multiple_of(j * 384, 16), 384)
            part[p, 0, to, :] = t[:, :128]
            part[p, 1, to, :] = t[:, 128:]
            return 0

        lax.fori_loop(0, 3, step, 0)

    def piece(p, zz):
        return pl.ds(pl.multiple_of(p * 32 + zz * PIECE, 16), PIECE)

    pr, pf, pl_ = mod(x + 1, NX), mod(x + 2, NX), mod(x + 3, NX)

    def xsum(s, zz):
        p, h, to = [
            (pf, 0, right), (pf, 1, left), (pr, 1, right), (pl_, 0, left), (pr, 0, right), (pl_, 1, left),
        ][s]
        return rc(
            part.at[p, h, piece(p, zz)], xr.at[s, zz], out.at[4], xs_r.at[0 if s < 2 else 1, zz], to
        )

    def far(zz):
        xsum(0, zz).start()
        xsum(1, zz).start()

    def near(zz):
        xsum(2, zz).start()
        xsum(3, zz).start()

    def hand_on(zz):
        all_here(xs_r.at[0, zz], xr.at[0:2, zz])
        for s, h, p in ((0, 0, pr), (1, 1, pl_)):
            rows = piece(p, zz)
            part[p, h, rows, :] = (
                part[p, h, rows, :].astype(F32) + xr[s, zz].astype(F32)
            ).astype(BF16)
            xsum(s + 4, zz).start()

    def root(zz):
        all_here(xs_r.at[1, zz], xr.at[2:6, zz])
        own = piece(x, zz)
        r32[:, 0:128] = part[x, 0, own, :].astype(F32) + (
            xr[3, zz].astype(F32) + xr[4, zz].astype(F32)
        )
        r32[:, 128:256] = part[x, 1, own, :].astype(F32) + (
            xr[2, zz].astype(F32) + xr[5, zz].astype(F32)
        )
        for kk in range(NY):
            for i in range(4):
                at = SLAB * i + OWN * kk
                frag[kk, OWN * i : OWN * (i + 1), :] = r32[at : at + OWN, :]
        for kk in range(NY):
            for h in range(2):
                ysend[zz, kk, h] = frag[kk][:, 128 * h : 128 * h + 128].astype(BF16)
        for n in range(4):
            ysum_copy(zz, n).start()

    def direct(zz):
        for n in (4, 5):
            ysum_copy(zz, n).start()

    def ysum_copy(zz, n):
        row = ysend.at[zz, kof((-3, 3, 4, 4, -1, 1, -2, 2)[n])]
        src, dst, to = [
            (row, ymid.at[zz, 0], -1),
            (row, ymid.at[zz, 1], 1),
            (row.at[0], yhalf.at[zz, 0], -2),
            (row.at[1], yhalf.at[zz, 1], 2),
            (row, yrecv.at[zz, 0], -1),
            (row, yrecv.at[zz, 1], 1),
            (row, yrecv.at[zz, 2], -2),
            (row, yrecv.at[zz, 3], 2),
        ][n]
        return rc(src, dst, out.at[5], ys_r.at[0 if n < 4 else 1, zz], at_y(y + NY + to))

    def mid(zz):
        all_here(ys_r.at[0, zz], ysend.at[zz, 0:3])
        for e in range(2):
            kk = kof((-2, 2)[e])
            for h in range(2):
                t = ysend[zz, kk, h].astype(F32) + ymid[zz, e, h].astype(F32)
                if h == e:
                    t = t + yhalf[zz, e].astype(F32)
                ysend[zz, kk, h] = t.astype(BF16)
            ysum_copy(zz, 6 + e).start()

    def zsum(zz):
        all_here(ys_r.at[1, zz], yrecv.at[zz])
        for h in range(2):
            t = ysend[zz, k, h].astype(F32)
            for e in range(4):
                t = t + yrecv[zz, e, h].astype(F32)
            ysum[0:48, 128 * h : 128 * h + 128] = t
        for i in range(4):
            zt = 4 * zz + i
            zsend[zt] = ysum[OWN * i : OWN * i + 16, :].astype(BF16)

            @pl.when(zt != z)
            def _():
                rc(zsend.at[zt], zrecv.at[z], out.at[6], into.at[1], dev(x, zt, k, c)).start()

            @pl.when(zt == z)
            def _():
                zrecv[zt] = zsend[zt]

    quarter(2).wait_recv()
    quarter(3).wait_recv()
    term(pf)
    far(0)
    quarter(0).wait_recv()
    term(pl_)
    quarter(1).wait_recv()
    term(pr)
    near(0)
    far(1)
    term(x)
    hand_on(0)
    far(2)
    near(1)

    all_here(into.at[0], chunk.at[0 : NX * NY - 1])
    for q in range(2):
        for e in range(2):
            for j in range(NY):
                at = SLAB * e + OWN * j
                zpack[at : at + OWN, :] = chunk[(2 * q + e) * NY + j].astype(F32)[:OWN]
        for h in range(2):
            zbuf[z, q, h] = zpack[:, 128 * h : 128 * h + 128].astype(BF16)

    def zslot(way, t):
        return mod(z + (NZ - t if way == 0 else t), NZ)

    def zhalves(way, t):
        return (0, 1) if t < 6 else (way,)

    def zcopy(way, t, h):
        at = zslot(way, t - 1)
        return rc(
            zbuf.at[at, odd, h], zbuf.at[at, odd, h], out.at[2], za_r.at[at, h],
            zright if way == 0 else zleft,
        )

    def zarrived(way, t, h):
        at = zslot(way, t)
        rc(
            zbuf.at[at, odd, h], zbuf.at[at, odd, h], out.at[2], za_r.at[at, h],
            zright if way == 0 else zleft,
        ).wait_recv()

    def across(way, t, h, q):
        at = zslot(way, t)
        return rc(
            zbuf.at[at, q, h], zbuf.at[at, q, h], out.at[3], zy_r.at[t - 1],
            (up, down, right, left)[h if t < 4 else 2 + h],
        )

    def place(at, q, h):
        v = zbuf[at, q, h].astype(F32)
        for e in range(2):
            to = pl.multiple_of((2 * q + e) * PLANE + at * SLAB, 8)
            w32[pl.ds(to, SLAB), 128 * h : 128 * h + 128] = v[e * SLAB : (e + 1) * SLAB]

    def zstep(t):
        for h in range(2):
            for way in range(2):
                if h not in zhalves(way, t):
                    continue
                zarrived(way, t, h)
                if t < 6 and h in zhalves(way, t + 1):
                    zcopy(way, t + 1, h).start()
                across(way, t, h, odd).start()
        for h in range(2):
            for way in range(2):
                if h in zhalves(way, t):
                    place(zslot(way, t), odd, h)

    def from_side(t):
        all_here(zy_r.at[t - 1], zbuf.at[0:2, 0] if t < 6 else zbuf.at[0, 0])
        for h in range(2):
            for way in range(2):
                if h in zhalves(way, t):
                    place(zslot(way, t), 1 - odd, h)

    for h in range(2):
        for way in range(2):
            zcopy(way, 1, h).start()
    for q in range(2):
        for h in range(2):
            place(z, q, h)
    zstep(1)
    hand_on(1)
    near(2)
    root(0)
    zstep(2)
    direct(0)
    hand_on(2)
    zstep(3)
    mid(0)
    root(1)
    zstep(4)
    direct(1)
    from_side(1)
    zsum(0)
    root(2)
    mid(1)
    zstep(5)
    direct(2)
    from_side(2)
    from_side(3)
    mid(2)
    zsum(1)
    zstep(6)
    from_side(4)

    def order(j):
        return jnp.where(odd == 0, j, NCH - 1 - j)

    def out_step(i, acc):
        j = order(i)
        at = pl.multiple_of(j * CH, CH)
        w = w32[pl.ds(at, CH), :].astype(BF16)
        acc = acc + jnp.dot(tok2[:, pl.ds(at, CH)], w, preferred_element_type=F32)
        g = lax.dot_general(cot2[:, mine], w, (((1,), (1,)), ((), ())), preferred_element_type=F32)
        gi32[j] = g[:T]
        gsend[j] = g[T:].astype(BF16)
        rc(gsend.at[j], grecv.at[j], out.at[7], sib_r.at[5 + j], sib).start()
        return acc

    def join(i):
        j = order(i)
        rc(gsend.at[j], grecv.at[j], out.at[7], sib_r.at[5 + j], sib).wait_recv()
        at = pl.multiple_of(j * CH, CH)
        gi[:, pl.ds(at, CH)] = (gi32[j] + grecv[j].astype(F32)).astype(BF16)

    acc = lax.fori_loop(0, 3, out_step, jnp.zeros((2 * T, HALF), F32), unroll=True)
    from_side(5)
    zsum(2)
    from_side(6)
    acc = lax.fori_loop(3, NCH, out_step, acc, unroll=True)
    other = pl.ds(pl.multiple_of((1 - c) * HALF, 128), HALF)
    keys[:, mine] = acc[:T].astype(BF16)
    ksend[...] = acc[T:].astype(BF16)
    ck = rc(ksend, krecv, sib_s.at[3], sib_r.at[3], sib)
    ck.start()
    for i in range(NCH):
        join(i)

    all_here(into.at[1], zrecv.at[0 : NZ - 1])
    s = zrecv[0].astype(F32)
    for j in range(1, NZ):
        s = s + zrecv[j].astype(F32)
    fin[c] = s
    cf = rc(fin.at[c], fin.at[c], sib_s.at[4], sib_r.at[4], sib)
    cf.start()
    ck.wait()
    keys[:, other] = krecv[...]

    all_sent(0, tok2.at[0:T, 0:D])
    all_sent(1, chunk.at[0 : NX * NY - 1])
    all_sent(2, zbuf.at[0:11, 0])
    all_sent(3, zbuf.at[0:11, 0])
    all_sent(4, xr)
    all_sent(5, ysend.at[:, 0:7])
    all_sent(6, zsend.at[0 : NZ - 1])
    all_sent(7, gsend)
    cf.wait()
    for r in range(OWN):
        rows = []
        for e in range(2):
            i = OWN * e + r
            rows.append(fin[i % 2, i // 2 : i // 2 + 1, :])
        gw[r : r + 1, :] = jnp.where(c == 0, rows[0], rows[1])


def store(keys, gi, gw, keys_out, gi_out, gw_out, sem):
    copies = [
        pltpu.make_async_copy(gi, gi_out, sem.at[0]),
        pltpu.make_async_copy(keys, keys_out, sem.at[1]),
        pltpu.make_async_copy(gw, gw_out, sem.at[2]),
    ]
    for copy in copies:
        copy.start()
    for copy in copies:
        copy.wait()


def per_device(tokens, cotangent, codes, scales):
    total = tokens.shape[0] * lax.axis_size("node") * lax.axis_size("local")
    dma = pltpu.SemaphoreType.DMA
    scratch = [
        pltpu.VMEM((2 * T, ROWS), BF16),
        pltpu.VMEM((2 * T, KV), BF16),
        pltpu.VMEM((2, 16, HALF), F32),
        pltpu.VMEM((16, HALF), F32),
        pltpu.VMEM((NX * NY, 16, HALF), BF16),
        pltpu.VMEM((2 * SLAB, HALF), F32),
        pltpu.VMEM((NZ, 2, 2, 2 * SLAB, 128), BF16),
        pltpu.VMEM((ROWS, HALF), F32),
        pltpu.VMEM((NX, 2, 1152, 128), BF16),
        pltpu.VMEM((6, 3, PIECE, 128), BF16),
        pltpu.VMEM((PIECE, HALF), F32),
        pltpu.VMEM((NY, 48, HALF), F32),
        pltpu.VMEM((3, NY, 2, 48, 128), BF16),
        pltpu.VMEM((3, 2, 2, 48, 128), BF16),
        pltpu.VMEM((3, 2, 48, 128), BF16),
        pltpu.VMEM((3, 4, 2, 48, 128), BF16),
        pltpu.VMEM((56, HALF), F32),
        pltpu.VMEM((NZ, 16, HALF), BF16),
        pltpu.VMEM((NZ, 16, HALF), BF16),
        pltpu.VMEM((2, 16, HALF), F32),
        pltpu.VMEM((NCH, T, CH), F32),
        pltpu.VMEM((NCH, T, CH), BF16),
        pltpu.VMEM((NCH, T, CH), BF16),
        pltpu.VMEM((T, HALF), BF16),
        pltpu.VMEM((T, HALF), BF16),
        pltpu.VMEM((OWN, HALF), BF16),
        pltpu.VMEM((1, OWN), BF16),
        dma((4,)),
        dma((5,)), dma((5 + NCH,)),
        dma((8,)), dma((2,)), dma((NX,)),
        dma((NZ, 2)), dma((6,)), dma((2, 3)), dma((2, 3)),
    ]
    vmem = pl.BlockSpec(memory_space=pltpu.VMEM)
    hbm = pl.BlockSpec(memory_space=pl.ANY)
    arrays = (tokens, cotangent, codes, scales.reshape(1, OWN))
    keys, gi, gw = pl.pallas_call(
        functools.partial(kernel, 1.0 / total**0.5),
        out_shape=(
            jax.ShapeDtypeStruct((T, KV), BF16),
            jax.ShapeDtypeStruct((T, D), BF16),
            jax.ShapeDtypeStruct((OWN, HALF), F32),
        ),
        in_specs=[hbm] * 4,
        out_specs=(vmem, vmem, vmem),
        scratch_shapes=scratch,
        compiler_params=pltpu.CompilerParams(
            collective_id=0, has_side_effects=True, vmem_limit_bytes=40 << 20
        ),
        name="fused",
    )(*[pltpu.with_memory_space_constraint(a, pltpu.HBM) for a in arrays])
    return pl.pallas_call(
        store,
        out_shape=(
            jax.ShapeDtypeStruct((T, KV), BF16),
            jax.ShapeDtypeStruct((T, D), BF16),
            jax.ShapeDtypeStruct((OWN, HALF), F32),
        ),
        in_specs=[vmem, vmem, vmem],
        out_specs=(hbm, hbm, hbm),
        scratch_shapes=[dma((3,))],
        name="store",
    )(*[pltpu.with_memory_space_constraint(a, pltpu.VMEM) for a in (keys, gi, gw)])


def solution(mesh):
    in_specs = (
        P(("node", "local"), None),
        P(("node", "local"), None),
        P(("node", "local"), None),
        P(("node", "local")),
    )
    out_specs = (P(("node", "local"), None), P(("node", "local"), None), P(("node", "local"), None))
    return jax.shard_map(
        per_device, mesh=mesh, in_specs=in_specs, out_specs=out_specs, check_vma=False
    )
```
